128 devices in a mesh: seq: 8 (over y_lo, z), head: 16 (over x, y_hi, core).
Axes of the slice: x: 4, y: 4 (y_hi: 2, y_lo: 2; y = y_hi * 2 + y_lo), z: 4, core: 2. Of those that a mesh axis runs over, the one named last changes fastest.
Arguments:
- tokens: bfloat16 [8, 1280, 3072], P('seq'), may hold values from -6 to 6
- spatial_modulation: float32 [3, 3072], replicated, may hold values from -3 to 3
- spatial_weights_in: bfloat16 [3072, 16, 384], P(None, 'head'), may hold values from -0.6 to 0.6, as said below
- spatial_weights_out: bfloat16 [16, 128, 3072], P('head'), may hold values from -0.5 to 0.5
- temporal_modulation: float32 [3, 3072], replicated, may hold values from -3 to 3
- temporal_weights_in: bfloat16 [3072, 16, 384], P(None, 'head'), may hold values from -0.6 to 0.6, as said below
- temporal_weights_out: bfloat16 [16, 128, 3072], P('head'), may hold values from -0.5 to 0.5
Outputs:
- updated_tokens: bfloat16 [8, 1280, 3072], P(None, ('seq', 'head'))
The draws below stay inside these ranges and needn't reach their ends.
Inputs may be any that keep to these rules, and one draw needn't show every extreme that they name: `spatial_weights_in`: query, key and value columns of each head, scaled for a fan-in of 3072. `temporal_weights_in`: query, key and value columns of each head, scaled for a fan-in of 3072.
All inputs are finite; a program needn't handle non-finite values.
Results may differ from the reference program's by a relative error of at most 0.034.
Values may be sent and summed in bfloat16 or wider, within the bound.
A program may use at most 128 MiB of HBM per device.

```python
import jax
import jax.numpy as jnp
from jax import lax

D = 3072
HD = 128
HEADS = 16
S = 1280
FRAMES = 8


def projection_pieces(key):
    query_key, other_key, value_key = jax.random.split(key, 3)
    query_base = jax.random.normal(query_key, (D, HEADS, HD), jnp.float32) * D ** (-0.5)
    other_base = jax.random.normal(other_key, (D, HEADS, HD), jnp.float32) * D ** (-0.5)
    value_base = jax.random.normal(value_key, (D, HEADS, HD), jnp.float32) * D ** (-0.5)
    return (query_base, other_base, value_base)


def assemble(query_part, key_part, value_part):
    joined = jnp.concatenate([query_part, key_part, value_part], axis=-1)
    return jnp.clip(joined, -0.59375, 0.59375).astype(jnp.bfloat16)


def draw_spatial_weights_in(key, part):
    key = jax.random.fold_in(key, 11)
    query_base, other_base, value_base = projection_pieces(key)
    query_part = query_base * 1.4
    key_part = other_base * 1.4
    return assemble(query_part, key_part, value_base)


def draw_temporal_weights_in(key, part):
    key = jax.random.fold_in(key, 23)
    query_base, other_base, value_base = projection_pieces(key)
    query_part = query_base * 1.4
    key_part = other_base * 1.4
    return assemble(query_part, key_part, value_base)


def steps_of(own_key, shape, shards, least, high):
    def one(axis_at, blocks):
        draws = jax.random.uniform(jax.random.fold_in(jax.random.fold_in(own_key, 6), axis_at), (blocks,), jnp.float32, least / len(shards), high / len(shards))
        return jnp.repeat(jnp.exp(draws), shape[axis_at] // blocks).reshape((-1,) + (1,) * (len(shape) - axis_at - 1))

    gain = one(*shards[0])
    for cut in shards[1:]:
        gain = gain * one(*cut)
    return gain


def bell_draw(rng, dims, scale, bound, pieces=(), dtype=jnp.bfloat16):
    level = steps_of(rng, dims, pieces, -0.22, 0.18) if pieces else 1.0
    entries = jax.random.normal(rng, dims, jnp.float32) * scale * level
    return jnp.minimum(jnp.maximum(entries, -bound), bound).astype(dtype)


def setup_inputs(seed: int = 0) -> dict:
    seeds = jax.random.split(jax.random.key(seed), 8)
    return {
        "tokens": bell_draw(seeds[0], (FRAMES, S, D), 1.0, 6.0, ((0, 8),)),
        "spatial_modulation": bell_draw(seeds[1], (3, D), 0.5, 3.0, (), jnp.float32),
        "spatial_weights_in": draw_spatial_weights_in(jax.random.fold_in(seeds[7], 71), 0),
        "spatial_weights_out": bell_draw(seeds[3], (HEADS, HD, D), HD ** -0.5, 0.5, ((0, 16),)),
        "temporal_modulation": bell_draw(seeds[4], (3, D), 0.5, 3.0, (), jnp.float32),
        "temporal_weights_in": draw_temporal_weights_in(jax.random.fold_in(seeds[7], 71), 0),
        "temporal_weights_out": bell_draw(seeds[6], (HEADS, HD, D), HD ** -0.5, 0.5, ((0, 16),)),
    }


def modulate(rows, modulation):
    values = rows.astype(jnp.float32)
    center = values - lax.optimization_barrier(jnp.mean(values, axis=-1, keepdims=True))
    spread = lax.optimization_barrier(jnp.mean(center * center, axis=-1, keepdims=True))
    normed = center * lax.rsqrt(spread + 1e-06)
    return (normed * (1.0 + modulation[1]) + modulation[0]).astype(jnp.bfloat16)

def project_in(normed, weights):
    frame_count, cell_count, feature_count = normed.shape
    joined = jnp.dot(normed.reshape(-1, feature_count), weights, preferred_element_type=jnp.float32)
    joined = joined.astype(jnp.bfloat16).reshape(frame_count, cell_count, -1)
    return (joined[..., :HD], joined[..., HD:2 * HD], joined[..., 2 * HD:])

def reference(tokens, spatial_modulation, spatial_weights_in, spatial_weights_out, temporal_modulation, temporal_weights_in, temporal_weights_out):
    score_scale = HD ** (-0.5)
    normed = modulate(tokens, spatial_modulation)

    def spatial_head(total, inputs):
        weights, outward = inputs
        queries, keys, values = project_in(normed, weights)
        scores = jnp.einsum('fsh,fth->fst', queries.astype(jnp.float32), keys.astype(jnp.float32)) * score_scale
        probs = jax.nn.softmax(scores, axis=-1).astype(jnp.bfloat16)
        attended = jnp.einsum('fst,fth->fsh', probs.astype(jnp.float32), values.astype(jnp.float32)).astype(jnp.bfloat16)
        term = jnp.dot(attended.reshape(-1, HD), outward, preferred_element_type=jnp.float32).astype(jnp.bfloat16)
        return (total + term.reshape(total.shape).astype(jnp.float32), None)
    start_total = jnp.zeros(tokens.shape, jnp.float32)
    summed, _ = lax.scan(spatial_head, start_total, (jnp.transpose(spatial_weights_in, (1, 0, 2)), spatial_weights_out))
    middle = (tokens.astype(jnp.float32) + spatial_modulation[2] * summed).astype(jnp.bfloat16)
    tnormed = modulate(middle, temporal_modulation)

    def temporal_head(total, inputs):
        weights, outward = inputs
        queries, keys, values = project_in(tnormed, weights)
        scores = jnp.einsum('fsh,gsh->sfg', queries.astype(jnp.float32), keys.astype(jnp.float32)) * score_scale
        probs = jax.nn.softmax(scores, axis=-1).astype(jnp.bfloat16)
        attended = jnp.einsum('sfg,gsh->sfh', probs.astype(jnp.float32), values.astype(jnp.float32)).astype(jnp.bfloat16)
        term = jnp.dot(attended.reshape(-1, HD), outward, preferred_element_type=jnp.float32).astype(jnp.bfloat16)
        return (total + term.reshape(total.shape).astype(jnp.float32), None)
    temporal_start = jnp.zeros((tokens.shape[1], tokens.shape[0], tokens.shape[2]), jnp.float32)
    tsummed, _ = lax.scan(temporal_head, temporal_start, (jnp.transpose(temporal_weights_in, (1, 0, 2)), temporal_weights_out))
    result = middle.astype(jnp.float32) + temporal_modulation[2] * jnp.swapaxes(tsummed, 0, 1)
    return result.astype(jnp.bfloat16)
```

```python
import functools

import jax
import jax.numpy as jnp
from jax import lax
from jax.experimental import pallas as pl
from jax.experimental.pallas import tpu as pltpu
from jax.sharding import PartitionSpec as P

BF = jnp.bfloat16
F32 = jnp.float32
MESH = pl.DeviceIdType.MESH
BLOCKS = 6
LOG2E = 1.4426950408889634


def dot(a, b):
    return jnp.dot(a, b, preferred_element_type=F32)


def dot_nt(a, b):
    return lax.dot_general(a, b, (((1,), (1,)), ((), ())), preferred_element_type=F32)


def iota(shape, axis):
    return lax.broadcasted_iota(jnp.int32, shape, axis)


def floor_div(v, n):
    return jnp.floor((v + 0.5) * (1.0 / n))


def remote(src, dst, send, recv, device):
    return pltpu.make_async_remote_copy(
        src_ref=src, dst_ref=dst, send_sem=send, recv_sem=recv,
        device_id=device, device_id_type=MESH,
    )


def query_rows(quarter, rows, cells):
    r = iota((rows, 1), 0).astype(F32)
    xx = floor_div(r, 80)
    r = r - xx * 80
    ss = floor_div(r, 10)
    ii = r - ss * 10
    p = ss * 160 + xx * 40 + ii + (quarter * 10).astype(F32)
    c = iota((1, cells), 1).astype(F32)
    return jnp.where(p == c, 1.0, 0.0).astype(BF)


def kernel(
    tok_in, smod, win_in, wo_in, tmod, wt_in, wto_in,
    out,
    tok, wi, wx, qb, kb, vx, att, cat, own_rows, wo, wt, wto,
    part, relay, got, shuf, shufr, gath, tnorm, qkv, tatt, part2, relay2, got2, res,
    local_sem, tok_sem, out_sem, win_sem, wsend, wrecv, asend, arecv,
    rsend, rrecv, ssend, srecv, gsend, grecv, rsend2, rrecv2,
):
    d = tok.shape[-1]
    nb = BLOCKS
    cb = d // nb
    hb = cb // 2
    s = lax.axis_index("seq")
    h = lax.axis_index("head")
    yl, z = s // 4, s % 4
    x, q = h // 4, h % 4
    yh, core = q // 2, q % 2
    right = (s, ((x + 1) % 4) * 4 + q)
    left = (s, ((x + 3) % 4) * 4 + q)
    quad = [None] + [
        (s, x * 4 + ((yh + r // 2) % 2) * 2 + (core + r) % 2) for r in (1, 2, 3)
    ]
    mate = quad[1]
    cross = ((1 - yl) * 4 + z, x * 4 + (1 - yh) * 2 + core)
    up = (yl * 4 + (z + 1) % 4, h)
    down = (yl * 4 + (z + 3) % 4, h)
    xr, xl, xo = (x + 1) % 4, (x + 3) % 4, (x + 2) % 4
    zu, zd, zo = (z + 1) % 4, (z + 3) % 4, (z + 2) % 4

    barrier = pltpu.get_barrier_semaphore()
    partners = [right, left] + quad[1:] + [cross] + [((s + j) % 8, h) for j in range(1, 8)]
    for device in partners:
        pl.semaphore_signal(barrier, inc=1, device_id=device, device_id_type=MESH)

    load_w = pltpu.make_async_copy(win_in, wi, win_sem)
    load_w.start()
    loads = [pltpu.make_async_copy(tok_in.at[i], tok.at[i], tok_sem.at[i]) for i in range(4)]
    for load in loads:
        load.start()
    own_loads = [
        pltpu.make_async_copy(src, dst.at[0], local_sem.at[i])
        for i, (src, dst) in enumerate(((wo_in, wo), (wt_in, wt), (wto_in, wto)))
    ]
    for load in own_loads:
        load.start()
    sends = []

    def go(copy):
        copy.start()
        sends.append(copy)
        return copy

    def weight_begin(w, src, buf):
        go(remote(src, buf.at[1], wsend.at[w, 0], wrecv.at[w, 0], mate))
        go(remote(src.at[z], buf.at[2, z], wsend.at[w, 1], wrecv.at[w, 1], cross))

    def weight_a(w, buf):
        piece = buf.at[2, z]
        remote(piece, piece, wsend.at[w, 1], wrecv.at[w, 1], cross).wait_recv()
        go(remote(piece, piece, wsend.at[w, 2], wrecv.at[w, 2], up))
        go(remote(piece, piece, wsend.at[w, 3], wrecv.at[w, 3], down))
        go(remote(piece, buf.at[3, z], wsend.at[w, 4], wrecv.at[w, 4], mate))

    def weight_b(w, buf):
        below, above = buf.at[2, zd], buf.at[2, zu]
        remote(below, below, wsend.at[w, 2], wrecv.at[w, 2], up).wait_recv()
        go(remote(below.at[0], below.at[0], wsend.at[w, 5], wrecv.at[w, 5], up))
        go(remote(below, buf.at[3, zd], wsend.at[w, 7], wrecv.at[w, 7], mate))
        remote(above, above, wsend.at[w, 3], wrecv.at[w, 3], down).wait_recv()
        go(remote(above.at[1], above.at[1], wsend.at[w, 6], wrecv.at[w, 6], down))
        go(remote(above, buf.at[3, zu], wsend.at[w, 8], wrecv.at[w, 8], mate))

    def weight_c(w, buf):
        far = buf.at[2, zo]
        remote(far.at[0], far.at[0], wsend.at[w, 5], wrecv.at[w, 5], up).wait_recv()
        go(remote(far.at[0], buf.at[3, zo, 0], wsend.at[w, 9], wrecv.at[w, 9], mate))
        remote(far.at[1], far.at[1], wsend.at[w, 6], wrecv.at[w, 6], down).wait_recv()
        go(remote(far.at[1], buf.at[3, zo, 1], wsend.at[w, 10], wrecv.at[w, 10], mate))

    def weight_end(w, src, buf):
        own_loads[w].wait()
        remote(src, buf.at[1], wsend.at[w, 0], wrecv.at[w, 0], mate).wait_recv()
        for k, piece in ((4, buf.at[3, z]), (7, buf.at[3, zd]), (8, buf.at[3, zu]),
                         (9, buf.at[3, zo, 0]), (10, buf.at[3, zo, 1])):
            remote(piece, piece, wsend.at[w, k], wrecv.at[w, k], mate).wait_recv()

    load_w.wait()
    m0 = smod[0:1, :]
    m0_high = m0.astype(BF).astype(F32)
    row = iota((16, d), 0)
    shift_rows = jnp.where(row == 0, m0_high, jnp.where(row == 1, m0 - m0_high, 0.0)).astype(BF)
    bias = jnp.sum(dot(shift_rows, wi[...]), axis=0, keepdims=True)

    def fold(i, _):
        rows = pl.ds(pl.multiple_of(i * 128, 128), 128)
        gain = jnp.broadcast_to(1.0 + smod[1:2, rows], (128, 128)).T
        for j in range(3):
            cols = slice(j * 128, (j + 1) * 128)
            wx[rows, cols] = (wi[rows, cols].astype(F32) * gain).astype(BF)
        wx[rows, 384:512] = jnp.ones((128, 128), BF)
        return 0

    lax.fori_loop(0, d // 128, fold, 0, unroll=4)
    colsum = dot(jnp.ones((16, d), BF), wx[:, 0:384])[0:1, :]

    pl.semaphore_wait(barrier, len(partners))
    weight_begin(0, wo_in, wo)
    weight_begin(1, wt_in, wt)

    def project(i, _):
        pltpu.make_async_copy(tok_in.at[i], tok.at[i], tok_sem.at[i]).wait()
        t = tok[i]
        raw = dot(t, wx[...])
        base = t[:, 0:1].astype(F32)
        squares = jnp.zeros((320, 128), F32)
        for j in range(d // 128):
            e = t[:, j * 128:(j + 1) * 128].astype(F32) - base
            squares = squares + e * e
        mean = raw[:, 384:385] * (1.0 / d)
        spread = jnp.sum(squares, axis=1, keepdims=True) * (1.0 / d) - (mean - base) * (mean - base)
        scale = lax.rsqrt(spread + 1e-06)
        full = ((raw[:, 0:384] - mean * colsum) * scale + bias).astype(BF)
        rows = pl.ds(pl.multiple_of(i * 320, 320), 320)
        qb[rows, :] = full[:, 0:128]
        kb[rows, :] = full[:, 128:256]
        vx[rows, 0:128] = full[:, 256:384]
        vx[rows, 128:256] = jnp.ones((320, 128), BF)
        return 0

    lax.fori_loop(0, 4, project, 0)
    weight_a(0, wo)

    score_scale = 128 ** (-0.5) * LOG2E

    def attend(r):
        quarter = ((yh + r // 2) % 2) * 2 + (core + r) % 2
        pick = query_rows(quarter, 320, 1280)
        queries = dot(pick, qb[...]).astype(BF)
        scores = dot_nt(queries, kb[...])
        top = jnp.max(scores, axis=1, keepdims=True)
        probs = jnp.exp2((scores - top) * score_scale).astype(BF)
        both = dot(probs, vx[...])
        result = (both[:, 0:128] / both[:, 128:256]).astype(BF)
        if r:
            att[r] = result
            go(remote(att.at[r], cat.at[r], asend.at[r], arecv.at[r], quad[r]))
        else:
            cat[0] = result

    attend(3)
    attend(2)
    weight_b(0, wo)
    attend(1)
    attend(0)
    weight_c(0, wo)

    first = h * 10
    start = jnp.minimum((first // 16) * 16, 128)
    skip = first - start
    r80 = iota((80, 1), 0).astype(F32)
    s80 = floor_div(r80, 10)
    target = s80 * 32 + (r80 - s80 * 10) + skip.astype(F32)
    pick_own = jnp.where(target == iota((1, 256), 1).astype(F32), 1.0, 0.0).astype(BF)
    flat = tok.reshape(1280, d)
    windows = jnp.concatenate(
        [flat[pl.ds(pl.multiple_of(k * 160 + start, 16), 32), :] for k in range(8)], axis=0
    )
    own_rows[...] = dot(pick_own, windows).astype(BF)

    t128 = iota((128, 1), 0).astype(F32)
    blk = floor_div(t128, 16)
    pos = t128 - blk * 16
    col80 = iota((1, 80), 1).astype(F32)
    spread_rows = jnp.where((pos < 10) & (blk * 10 + pos == col80), 1.0, 0.0).astype(BF)
    i80 = floor_div(r80, 8)
    f80 = r80 - i80 * 8
    dense_rows = jnp.where(f80 * 16 + i80 == iota((1, 128), 1).astype(F32), 1.0, 0.0).astype(BF)

    def ring_compute(b, lhs, w, buf):
        cols = pl.ds(b * cb, cb)
        block = w[:, :, :, :, cols].reshape(512, cb)
        buf[b] = dot(lhs, block).astype(BF).reshape(4, 80, cb)

    def ring_first(b, buf, rel, rec, ss, rs):
        lo, hi = pl.ds(0, hb), pl.ds(hb, hb)
        go(remote(buf.at[b, xo, :, lo], rel.at[b, 0], ss.at[b, 0], rs.at[b, 0], right))
        go(remote(buf.at[b, xo, :, hi], rel.at[b, 1], ss.at[b, 1], rs.at[b, 1], left))
        go(remote(buf.at[b, xr, :, hi], rec.at[b, 0, 1], ss.at[b, 2], rs.at[b, 2], right))
        go(remote(buf.at[b, xl, :, lo], rec.at[b, 1, 0], ss.at[b, 3], rs.at[b, 3], left))

    def ring_second(b, buf, rel, rec, ss, rs):
        lo, hi = pl.ds(0, hb), pl.ds(hb, hb)
        remote(rel.at[b, 0], rel.at[b, 0], ss.at[b, 0], rs.at[b, 0], right).wait_recv()
        rel[b, 0] = (rel[b, 0].astype(F32) + buf[b, xr, :, lo].astype(F32)).astype(BF)
        go(remote(rel.at[b, 0], rec.at[b, 0, 0], ss.at[b, 4], rs.at[b, 4], right))
        remote(rel.at[b, 1], rel.at[b, 1], ss.at[b, 1], rs.at[b, 1], left).wait_recv()
        rel[b, 1] = (rel[b, 1].astype(F32) + buf[b, xl, :, hi].astype(F32)).astype(BF)
        go(remote(rel.at[b, 1], rec.at[b, 1, 1], ss.at[b, 5], rs.at[b, 5], left))

    def ring_last(b, buf, rec, ss, rs):
        for k, (side, half) in ((2, (0, 1)), (3, (1, 0)), (4, (0, 0)), (5, (1, 1))):
            remote(rec.at[b, side, half], rec.at[b, side, half], ss.at[b, k], rs.at[b, k], right).wait_recv()
        own = buf[b, x].astype(F32)
        halves = [
            own[:, k * hb:(k + 1) * hb] + rec[b, 0, k].astype(F32) + rec[b, 1, k].astype(F32)
            for k in range(2)
        ]
        return jnp.concatenate(halves, axis=1)

    def swap_send(b):
        total = ring_last(b, part, got, rsend, rrecv)
        cols = pl.ds(b * cb, cb)
        middle = (own_rows[:, cols].astype(F32) + smod[2:3, cols] * total).astype(BF)
        padded = dot(spread_rows, middle).astype(BF).reshape(8, 16, cb)
        shuf[b] = padded
        for j in range(1, 8):
            to = (s + j) % 8
            go(remote(shuf.at[b, to], shufr.at[b, s], ssend.at[b, j], srecv.at[b, j], (to, h)))
        shufr[b, s] = shuf[b, s]

    def gather_send(b):
        for j in range(1, 8):
            piece = shufr.at[b, (s + 8 - j) % 8]
            remote(piece, piece, ssend.at[b, j], srecv.at[b, j], right).wait_recv()
        gath[b, x] = dot(dense_rows, shufr[b].reshape(128, cb)).astype(BF)
        mine = gath.at[b, x]
        go(remote(mine, mine, gsend.at[b, 0], grecv.at[b, 0], right))
        go(remote(mine, mine, gsend.at[b, 1], grecv.at[b, 1], left))

    def gather_relay(b):
        from_left, from_right = gath.at[b, xl], gath.at[b, xr]
        remote(from_left, from_left, gsend.at[b, 0], grecv.at[b, 0], right).wait_recv()
        piece = gath.at[b, xl, :, pl.ds(0, hb)]
        go(remote(piece, piece, gsend.at[b, 2], grecv.at[b, 2], right))
        remote(from_right, from_right, gsend.at[b, 1], grecv.at[b, 1], left).wait_recv()
        piece = gath.at[b, xr, :, pl.ds(hb, hb)]
        go(remote(piece, piece, gsend.at[b, 3], grecv.at[b, 3], left))

    def gather_end(b):
        lo, hi = gath.at[b, xo, :, pl.ds(0, hb)], gath.at[b, xo, :, pl.ds(hb, hb)]
        remote(lo, lo, gsend.at[b, 2], grecv.at[b, 2], right).wait_recv()
        remote(hi, hi, gsend.at[b, 3], grecv.at[b, 3], left).wait_recv()

    for r in (1, 2, 3):
        remote(att.at[r], cat.at[r], asend.at[r], arecv.at[r], quad[r]).wait_recv()
    weight_end(0, wo_in, wo)
    lhs = jnp.concatenate([cat[r] for r in range(4)], axis=1)

    for t in range(nb + 5):
        if t < nb:
            ring_compute(t, lhs, wo, part)
            ring_first(t, part, relay, got, rsend, rrecv)
        if 0 <= t - 1 < nb:
            ring_second(t - 1, part, relay, got, rsend, rrecv)
        if t == 1:
            weight_begin(2, wto_in, wto)
            weight_a(1, wt)
        if 0 <= t - 2 < nb:
            swap_send(t - 2)
        if 0 <= t - 3 < nb:
            gather_send(t - 3)
        if t == 4:
            weight_b(1, wt)
        if 0 <= t - 4 < nb:
            gather_relay(t - 4)
        if t == nb:
            weight_c(1, wt)
        if 0 <= t - 5 < nb:
            gather_end(t - 5)

    weight_a(2, wto)
    total = jnp.zeros((320, 128), F32)
    squares = jnp.zeros((320, 128), F32)
    base = gath[0, :, :, 0:128].reshape(320, 128)[:, 0:1].astype(F32)
    for b in range(nb):
        rows = gath[b].reshape(320, cb)
        for j in range(cb // 128):
            e = rows[:, j * 128:(j + 1) * 128].astype(F32) - base
            total = total + e
            squares = squares + e * e
    off = jnp.sum(total, axis=1, keepdims=True) * (1.0 / d)
    spread = jnp.sum(squares, axis=1, keepdims=True) * (1.0 / d) - off * off
    scale = lax.rsqrt(spread + 1e-06)
    mean = base + off
    for b in range(nb):
        cols = slice(b * cb, (b + 1) * cb)
        rows = gath[b].reshape(320, cb).astype(F32)
        tnorm[:, cols] = ((rows - mean) * scale * (1.0 + tmod[1:2, cols]) + tmod[0:1, cols]).astype(BF)
    weight_b(2, wto)
    weight_end(1, wt_in, wt)

    def temporal_project(j, _):
        qkv[j] = dot(tnorm[...], wt[j].reshape(d, 384)).astype(BF)
        return 0

    lax.fori_loop(0, 4, temporal_project, 0)
    weight_c(2, wto)
    same = (iota((320, 320), 0) >> 3) == (iota((320, 320), 1) >> 3)
    for j in range(4):
        scores = dot_nt(qkv[j, :, 0:128], qkv[j, :, 128:256])
        scores = jnp.where(same, scores, -1e30)
        top = jnp.max(scores, axis=1, keepdims=True)
        probs = jnp.exp2((scores - top) * score_scale)
        probs = (probs / jnp.sum(probs, axis=1, keepdims=True)).astype(BF)
        tatt[:, j * 128:(j + 1) * 128] = dot(probs, qkv[j, :, 256:384]).astype(BF)
    weight_end(2, wto_in, wto)
    lhs = tatt[...]

    stores = []
    for t in range(nb + 2):
        if t < nb:
            ring_compute(t, lhs, wto, part2)
            ring_first(t, part2, relay2, got2, rsend2, rrecv2)
        if 0 <= t - 1 < nb:
            ring_second(t - 1, part2, relay2, got2, rsend2, rrecv2)
        if 0 <= t - 2 < nb:
            b = t - 2
            total = ring_last(b, part2, got2, rsend2, rrecv2)
            cols = pl.ds(b * cb, cb)
            res[b] = (gath[b, x].astype(F32) + tmod[2:3, cols] * total).astype(BF)
            store = pltpu.make_async_copy(res.at[b], out.at[:, cols], out_sem.at[b])
            store.start()
            stores.append(store)
    for store in stores:
        store.wait()
    for copy in sends:
        copy.wait_send()


def shards(
    tokens, spatial_modulation, spatial_weights_in, spatial_weights_out,
    temporal_modulation, temporal_weights_in, temporal_weights_out,
):
    d = tokens.shape[-1]
    nb, cb = BLOCKS, d // BLOCKS
    hb = cb // 2
    dma = pltpu.SemaphoreType.DMA
    any_space = pl.BlockSpec(memory_space=pl.ANY)
    vmem = pl.BlockSpec(memory_space=pltpu.VMEM)
    out_weights = pltpu.VMEM((4, 4, 2, 16, d), BF)
    ring = [
        pltpu.VMEM((nb, 4, 80, cb), BF),
        pltpu.VMEM((nb, 2, 80, hb), BF),
        pltpu.VMEM((nb, 2, 2, 80, hb), BF),
    ]
    result = pl.pallas_call(
        kernel,
        out_shape=jax.ShapeDtypeStruct((80, d), BF),
        in_specs=[any_space, vmem, any_space, any_space, vmem, any_space, any_space],
        out_specs=any_space,
        scratch_shapes=[
            pltpu.VMEM((4, 320, d), BF),
            pltpu.VMEM((d, 384), BF),
            pltpu.VMEM((d, 512), BF),
            pltpu.VMEM((1280, 128), BF),
            pltpu.VMEM((1280, 128), BF),
            pltpu.VMEM((1280, 256), BF),
            pltpu.VMEM((4, 320, 128), BF),
            pltpu.VMEM((4, 320, 128), BF),
            pltpu.VMEM((80, d), BF),
            out_weights,
            pltpu.VMEM((4, 4, 2, d // 8, 384), BF),
            out_weights,
            *ring,
            pltpu.VMEM((nb, 8, 16, cb), BF),
            pltpu.VMEM((nb, 8, 16, cb), BF),
            pltpu.VMEM((nb, 4, 80, cb), BF),
            pltpu.VMEM((320, d), BF),
            pltpu.VMEM((4, 320, 384), BF),
            pltpu.VMEM((320, 512), BF),
            *ring,
            pltpu.VMEM((nb, 80, cb), BF),
            dma((3,)), dma((4,)), dma((nb,)), dma(()),
            dma((3, 11)), dma((3, 11)),
            dma((4,)), dma((4,)),
            dma((nb, 6)), dma((nb, 6)),
            dma((nb, 8)), dma((nb, 8)),
            dma((nb, 4)), dma((nb, 4)),
            dma((nb, 6)), dma((nb, 6)),
        ],
        compiler_params=pltpu.CompilerParams(
            collective_id=0, has_side_effects=True, vmem_limit_bytes=60 * 1024 * 1024
        ),
        cost_estimate=pl.CostEstimate(
            flops=9_000_000_000, bytes_accessed=16_000_000, transcendentals=2_000_000
        ),
    )(
        tokens.reshape(4, 320, d),
        spatial_modulation,
        jnp.transpose(spatial_weights_in, (1, 0, 2)).reshape(d, 384),
        spatial_weights_out.reshape(4, 2, 16, d),
        temporal_modulation,
        jnp.transpose(temporal_weights_in, (1, 0, 2)).reshape(4, 2, d // 8, 384),
        temporal_weights_out.reshape(4, 2, 16, d),
    )
    return jnp.transpose(result.reshape(10, 8, d), (1, 0, 2))


def solution(mesh):
    placed = (
        P("seq", None, None),
        P(),
        P(None, "head", None),
        P("head", None, None),
        P(),
        P(None, "head", None),
        P("head", None, None),
    )
    return jax.shard_map(
        shards,
        mesh=mesh,
        in_specs=placed,
        out_specs=P(None, ("seq", "head"), None),
        check_vma=False,
    )
```

```python
import functools

import jax
import jax.numpy as jnp
from jax import lax
from jax.experimental import pallas as pl
from jax.experimental.pallas import tpu as pltpu
from jax.sharding import PartitionSpec as P

BF = jnp.bfloat16
F32 = jnp.float32
MESH = pl.DeviceIdType.MESH
BLOCKS = 5
LOG2E = 1.4426950408889634
TICKS = (
    (0, (1, 0)), (0, (1, 1)), (1, (1, 2)), (1, (1, 3)), (2, (1,)), (3, (2, 0)), (3, (2, 1)), (4, (2,)),
)


def dot(a, b):
    return jnp.dot(a, b, preferred_element_type=F32)


def dot_nt(a, b):
    return lax.dot_general(a, b, (((1,), (1,)), ((), ())), preferred_element_type=F32)


def iota(shape, axis):
    return lax.broadcasted_iota(jnp.int32, shape, axis)


def one_hot(hit):
    return jnp.where(hit, 1.0, 0.0).astype(BF)


def remote(src, dst, send, recv, device):
    return pltpu.make_async_remote_copy(
        src_ref=src, dst_ref=dst, send_sem=send, recv_sem=recv,
        device_id=device, device_id_type=MESH,
    )


def kernel(
    tok_in, smod, win_in, wo_in, tmod, wt_in, wto_in,
    out,
    tok, wi, wx, qb, kb, vx, att, cat, own_rows, wo, wt, wto,
    part, relay, got, shuf, shufr, gath, part2, relay2, got2, res,
    local_sem, tok_sem, out_sem, win_sem, wsend, wrecv, asend, arecv,
    rsend, rrecv, ssend, srecv, gsend, grecv, rsend2, rrecv2,
):
    d = tok.shape[-1]
    nb = BLOCKS
    hb = d // 2
    eighth = d // 8
    s = lax.axis_index("seq")
    h = lax.axis_index("head")
    yl, z = s // 4, s % 4
    x, q = h // 4, h % 4
    yh, core = q // 2, q % 2
    right = (s, ((x + 1) % 4) * 4 + q)
    left = (s, ((x + 3) % 4) * 4 + q)
    quarters = [((yh + r // 2) % 2) * 2 + (core + r) % 2 for r in range(4)]
    quad = [(s, x * 4 + k) for k in quarters]
    mate = quad[1]
    cross = ((1 - yl) * 4 + z, x * 4 + (1 - yh) * 2 + core)
    beside = ((1 - yl) * 4 + z, h)
    up = (yl * 4 + (z + 1) % 4, h)
    down = (yl * 4 + (z + 3) % 4, h)
    xr, xl, xo = (x + 1) % 4, (x + 3) % 4, (x + 2) % 4
    zu, zd, zo = (z + 1) % 4, (z + 3) % 4, (z + 2) % 4

    barrier = pltpu.get_barrier_semaphore()
    partners = [right, left] + quad[1:] + [cross] + [((s + j) % 8, h) for j in range(1, 8)]
    for device in partners:
        pl.semaphore_signal(barrier, inc=1, device_id=device, device_id_type=MESH)

    load_w = pltpu.make_async_copy(win_in, wi, win_sem)
    load_w.start()
    for i in range(4):
        pltpu.make_async_copy(tok_in.at[i], tok.at[i], tok_sem.at[i]).start()
    weights = ((wo_in, wo), (wt_in, wt), (wto_in, wto))
    own_loads = [
        pltpu.make_async_copy(src, dst.at[0], local_sem.at[i]) for i, (src, dst) in enumerate(weights)
    ]
    for load in own_loads:
        load.start()

    def pieces(w):
        src, buf = weights[w]
        n = buf.shape[2]
        return src, buf, n, n // 2

    def copy_of(w, kind, k, piece, to, device):
        return remote(piece, to, wsend.at[w, kind, k], wrecv.at[w, kind, k], device)

    def weight_begin(w):
        src, buf, n, m = pieces(w)
        copy_of(w, 0, 0, src, buf.at[1], mate).start()
        for k in range(n):
            copy_of(w, 1, k, src.at[z, k], buf.at[2, z, k], cross).start()
        half = pl.ds((1 - yl) * m, m)
        copy_of(w, 2, 0, src.at[zo, half], buf.at[2, zo, half], cross).start()

    def weight_quarter(w, k):
        _, buf, _, _ = pieces(w)
        piece = buf.at[2, z, k]
        copy_of(w, 1, k, piece, piece, cross).wait_recv()
        copy_of(w, 3, k, piece, piece, up).start()
        copy_of(w, 4, k, piece, piece, down).start()
        copy_of(w, 5, k, piece, buf.at[3, z, k], mate).start()

    def weight_half(w):
        _, buf, _, m = pieces(w)
        half = pl.ds(yl * m, m)
        piece = buf.at[2, zo, half]
        copy_of(w, 2, 0, piece, piece, cross).wait_recv()
        copy_of(w, 6, 0, piece, piece, beside).start()
        copy_of(w, 7, 0, piece, buf.at[3, zo, half], mate).start()

    def weight_rest(w):
        _, buf, n, m = pieces(w)
        for kind, zz in ((3, zd), (4, zu)):
            for k in range(n):
                piece = buf.at[2, zz, k]
                copy_of(w, kind, k, piece, piece, up).wait_recv()
            copy_of(w, 8, kind - 3, buf.at[2, zz], buf.at[3, zz], mate).start()
        half = pl.ds((1 - yl) * m, m)
        piece = buf.at[2, zo, half]
        copy_of(w, 6, 0, piece, piece, beside).wait_recv()
        copy_of(w, 8, 2, piece, buf.at[3, zo, half], mate).start()

    def weight_end(w):
        src, buf, n, m = pieces(w)
        own_loads[w].wait()
        copy_of(w, 0, 0, src, buf.at[1], mate).wait_recv()
        for k in range(n):
            piece = buf.at[3, z, k]
            copy_of(w, 5, k, piece, piece, mate).wait_recv()
        mine = buf.at[3, zo, pl.ds(yl * m, m)]
        copy_of(w, 7, 0, mine, mine, mate).wait_recv()
        for k, zz in ((0, zd), (1, zu)):
            piece = buf.at[3, zz]
            copy_of(w, 8, k, piece, piece, mate).wait_recv()
        other = buf.at[3, zo, pl.ds((1 - yl) * m, m)]
        copy_of(w, 8, 2, other, other, mate).wait_recv()

    def weight_sent(w):
        src, buf, n, m = pieces(w)
        piece, half, whole = buf.at[2, z, 0], buf.at[2, zo, pl.ds(yl * m, m)], buf.at[2, z]
        copy_of(w, 0, 0, src, buf.at[1], mate).wait_send()
        for kind, device in ((1, cross), (3, up), (4, down), (5, mate)):
            for k in range(n):
                copy_of(w, kind, k, piece, piece, device).wait_send()
        for kind, device in ((2, cross), (6, beside), (7, mate)):
            copy_of(w, kind, 0, half, half, device).wait_send()
        for k in range(2):
            copy_of(w, 8, k, whole, whole, mate).wait_send()
        copy_of(w, 8, 2, half, half, mate).wait_send()

    load_w.wait()
    m0 = smod[0:1, :]
    m0_high = m0.astype(BF).astype(F32)
    row = iota((16, d), 0)
    shift_rows = jnp.where(row == 0, m0_high, jnp.where(row == 1, m0 - m0_high, 0.0)).astype(BF)
    bias = jnp.sum(dot(shift_rows, wi[...]), axis=0, keepdims=True)

    def fold(i, _):
        rows = pl.ds(pl.multiple_of(i * 128, 128), 128)
        gain = jnp.broadcast_to(1.0 + smod[1:2, rows], (128, 128)).T
        for j in range(3):
            cols = slice(j * 128, (j + 1) * 128)
            wx[rows, cols] = (wi[rows, cols].astype(F32) * gain).astype(BF)
        wx[rows, 384:512] = jnp.ones((128, 128), BF)
        return 0

    lax.fori_loop(0, d // 128, fold, 0, unroll=4)
    colsum = dot(jnp.ones((16, d), BF), wx[:, 0:384])[0:1, :]

    def project(i, _):
        pltpu.make_async_copy(tok_in.at[i], tok.at[i], tok_sem.at[i]).wait()

        @pl.when(i == 2)
        def _():
            pl.semaphore_wait(barrier, len(partners))
            for w in range(3):
                weight_begin(w)

        t = tok[i]
        raw = dot(t, wx[...])
        base = t[:, 0:1].astype(F32)
        squares = jnp.zeros((320, 128), F32)
        for j in range(d // 128):
            e = t[:, j * 128:(j + 1) * 128].astype(F32) - base
            squares = squares + e * e
        mean = raw[:, 384:385] * (1.0 / d)
        spread = jnp.sum(squares, axis=1, keepdims=True) * (1.0 / d) - (mean - base) * (mean - base)
        scale = lax.rsqrt(spread + 1e-06)
        full = ((raw[:, 0:384] - mean * colsum) * scale + bias).astype(BF)
        rows = pl.ds(pl.multiple_of(i * 320, 320), 320)
        qb[rows, :] = full[:, 0:128]
        kb[rows, :] = full[:, 128:256]
        vx[rows, 0:128] = full[:, 256:384]
        vx[rows, 128:256] = jnp.ones((320, 128), BF)
        return 0

    lax.fori_loop(0, 4, project, 0)

    score_scale = 128 ** (-0.5) * LOG2E

    r256 = iota((256, 1), 0)
    spot = ((r256 >> 1) & 7) * 160 + ((r256 >> 4) & 3) * 40 + (r256 >> 6) * 10 + (r256 & 1)
    cells = iota((1, 1280), 1)

    def attend(b, _):
        queries = dot(one_hot(spot + 2 * b == cells), qb[...]).astype(BF)
        scores = dot_nt(queries, kb[...])
        top = jnp.max(scores, axis=1, keepdims=True)
        probs = jnp.exp2((scores - top) * score_scale).astype(BF)
        both = dot(probs, vx[...])
        att[b] = (both[:, 0:128] / both[:, 128:256]).astype(BF).reshape(4, 64, 128)
        for r in (2, 3, 1):
            remote(att.at[b, quarters[r]], cat.at[b, r], asend.at[b, r], arecv.at[b, r], quad[r]).start()

        @pl.when(b == 2)
        def _():
            weight_quarter(0, 0)
            weight_quarter(0, 1)

        return 0

    lax.fori_loop(0, nb, attend, 0)
    weight_half(0)

    first = h * 10
    start = jnp.minimum((first // 16) * 16, 128)
    skip = first - start
    r80 = iota((80, 1), 0)
    target = ((r80 >> 1) & 7) * 32 + (r80 >> 4) * 2 + (r80 & 1) + skip
    flat = tok.reshape(1280, d)
    windows = jnp.concatenate(
        [flat[pl.ds(pl.multiple_of(k * 160 + start, 16), 32), :] for k in range(8)], axis=0
    )
    own_rows[...] = dot(one_hot(target == iota((1, 256), 1)), windows).astype(BF)

    r128 = iota((128, 1), 0)
    c128 = iota((1, 128), 1)
    to_send = one_hot((r128 & 7) * 16 + (r128 >> 4) * 2 + ((r128 >> 3) & 1) == c128)
    from_recv = one_hot((r128 & 7) * 16 + ((r128 >> 3) & 1) * 8 + (r128 >> 4) == c128)
    lo, hi = pl.ds(0, hb), pl.ds(hb, hb)

    def ring_first(b, buf, rel, rec, ss, rs):
        remote(buf.at[b, xo, :, lo], rel.at[b, 0], ss.at[b, 0], rs.at[b, 0], right).start()
        remote(buf.at[b, xo, :, hi], rel.at[b, 1], ss.at[b, 1], rs.at[b, 1], left).start()
        remote(buf.at[b, xr, :, hi], rec.at[b, 0, 1], ss.at[b, 2], rs.at[b, 2], right).start()
        remote(buf.at[b, xl, :, lo], rec.at[b, 1, 0], ss.at[b, 3], rs.at[b, 3], left).start()

    def ring_second(b, buf, rel, rec, ss, rs):
        remote(rel.at[b, 0], rel.at[b, 0], ss.at[b, 0], rs.at[b, 0], right).wait_recv()
        rel[b, 0] = (rel[b, 0].astype(F32) + buf[b, xr, :, lo].astype(F32)).astype(BF)
        remote(rel.at[b, 0], rec.at[b, 0, 0], ss.at[b, 4], rs.at[b, 4], right).start()
        remote(rel.at[b, 1], rel.at[b, 1], ss.at[b, 1], rs.at[b, 1], left).wait_recv()
        rel[b, 1] = (rel[b, 1].astype(F32) + buf[b, xl, :, hi].astype(F32)).astype(BF)
        remote(rel.at[b, 1], rec.at[b, 1, 1], ss.at[b, 5], rs.at[b, 5], left).start()

    def ring_last(b, buf, rec, ss, rs):
        for k, side, half in ((2, 0, 1), (3, 1, 0), (4, 0, 0), (5, 1, 1)):
            piece = rec.at[b, side, half]
            remote(piece, piece, ss.at[b, k], rs.at[b, k], right).wait_recv()
        own = buf[b, x].astype(F32)
        halves = [
            own[:, k * hb:(k + 1) * hb] + rec[b, 0, k].astype(F32) + rec[b, 1, k].astype(F32)
            for k in range(2)
        ]
        return jnp.concatenate(halves, axis=1)

    def ring_sent(b, rel, ss, rs):
        for k in range(6):
            remote(rel.at[b, 0], rel.at[b, 0], ss.at[b, k], rs.at[b, k], right).wait_send()

    def sum_begin(b):
        for r in (1, 2, 3):
            remote(cat.at[b, r], cat.at[b, r], asend.at[b, r], arecv.at[b, r], quad[r]).wait_recv()
        lhs = jnp.concatenate([att[b, q], cat[b, 1], cat[b, 2], cat[b, 3]], axis=1)
        part[b] = dot(lhs, wo[...].reshape(512, d)).astype(BF).reshape(4, 16, d)
        ring_first(b, part, relay, got, rsend, rrecv)

    def swap_send(b):
        total = ring_last(b, part, got, rsend, rrecv)
        rows = own_rows[pl.ds(pl.multiple_of(b * 16, 16), 16), :]
        middle = (rows.astype(F32) + smod[2:3, :] * total).astype(BF)
        stacked = jnp.concatenate([middle[:, k * eighth:(k + 1) * eighth] for k in range(8)], axis=0)
        shuf[b] = dot(to_send, stacked).astype(BF).reshape(8, 16, eighth)
        for j in (4, 1, 7, 5, 3, 2, 6):
            to = (s + j) % 8
            remote(shuf.at[b, to], shufr.at[b, s], ssend.at[b, j], srecv.at[b, j], (to, h)).start()
        shufr[b, s] = shuf[b, s]

    def gather_send(b):
        for j in range(1, 8):
            piece = shufr.at[b, (s + 8 - j) % 8]
            remote(piece, piece, ssend.at[b, j], srecv.at[b, j], right).wait_recv()
        rows = dot(from_recv, shufr[b].reshape(128, eighth)).astype(BF)
        gath[b, x] = jnp.concatenate([rows[k * 16:(k + 1) * 16, :] for k in range(8)], axis=1)
        mine = gath.at[b, x]
        remote(mine, mine, gsend.at[b, 0], grecv.at[b, 0], right).start()
        remote(mine, mine, gsend.at[b, 1], grecv.at[b, 1], left).start()

    def gather_relay(b):
        from_left, from_right = gath.at[b, xl], gath.at[b, xr]
        remote(from_left, from_left, gsend.at[b, 0], grecv.at[b, 0], right).wait_recv()
        piece = gath.at[b, xl, :, lo]
        remote(piece, piece, gsend.at[b, 2], grecv.at[b, 2], right).start()
        remote(from_right, from_right, gsend.at[b, 1], grecv.at[b, 1], left).wait_recv()
        piece = gath.at[b, xr, :, hi]
        remote(piece, piece, gsend.at[b, 3], grecv.at[b, 3], left).start()

    same = (iota((64, 64), 0) >> 3) == (iota((64, 64), 1) >> 3)

    def temporal(b):
        far = gath.at[b, xo]
        remote(far.at[:, lo], far.at[:, lo], gsend.at[b, 2], grecv.at[b, 2], right).wait_recv()
        remote(far.at[:, hi], far.at[:, hi], gsend.at[b, 3], grecv.at[b, 3], left).wait_recv()
        rows = gath[b].reshape(64, d).astype(F32)
        center = rows - jnp.sum(rows, axis=1, keepdims=True) * (1.0 / d)
        spread = jnp.sum(center * center, axis=1, keepdims=True) * (1.0 / d)
        scale = lax.rsqrt(spread + 1e-06)
        normed = (center * scale * (1.0 + tmod[1:2, :]) + tmod[0:1, :]).astype(BF)

        @pl.when(b == 0)
        def _():
            weight_rest(1)
            weight_end(1)

        attended = []
        for j in range(4):
            joined = dot(normed, wt[j].reshape(d, 384)).astype(BF)
            scores = dot_nt(joined[:, 0:128], joined[:, 128:256])
            scores = jnp.where(same, scores, -1e30)
            top = jnp.max(scores, axis=1, keepdims=True)
            probs = jnp.exp2((scores - top) * score_scale)
            probs = (probs / jnp.sum(probs, axis=1, keepdims=True)).astype(BF)
            attended.append(dot(probs, joined[:, 256:384]).astype(BF))

        @pl.when(b == 0)
        def _():
            weight_rest(2)
            weight_end(2)

        lhs = jnp.concatenate(attended, axis=1)
        part2[b] = dot(lhs, wto[...].reshape(512, d)).astype(BF).reshape(4, 16, d)
        ring_first(b, part2, relay2, got2, rsend2, rrecv2)

    def finish(b):
        total = ring_last(b, part2, got2, rsend2, rrecv2)
        res[b] = (gath[b, x].astype(F32) + tmod[2:3, :] * total).astype(BF)
        rows = pl.ds(pl.multiple_of(b * 16, 16), 16)
        pltpu.make_async_copy(res.at[b], out.at[rows, :], out_sem.at[b]).start()

    weight_rest(0)
    weight_end(0)

    stages = (
        sum_begin,
        lambda b: ring_second(b, part, relay, got, rsend, rrecv),
        swap_send,
        gather_send,
        gather_relay,
        temporal,
        lambda b: ring_second(b, part2, relay2, got2, rsend2, rrecv2),
        finish,
    )

    def tick(t, _):
        for k, stage in enumerate(stages):
            @pl.when((t >= k) & (t < k + nb))
            def _(stage=stage, k=k):
                stage(t - k)

        for when, move in TICKS:
            @pl.when(t == when)
            def _(move=move):
                if len(move) == 1:
                    weight_half(*move)
                else:
                    weight_quarter(*move)

        return 0

    lax.fori_loop(0, nb + len(stages) - 1, tick, 0)

    for b in range(nb):
        pltpu.make_async_copy(res.at[b], out.at[pl.ds(b * 16, 16), :], out_sem.at[b]).wait()

    def sent(b, _):
        for r in (1, 2, 3):
            remote(cat.at[b, r], cat.at[b, r], asend.at[b, r], arecv.at[b, r], quad[r]).wait_send()
        ring_sent(b, relay, rsend, rrecv)
        ring_sent(b, relay2, rsend2, rrecv2)
        for j in range(1, 8):
            piece = shuf.at[b, 0]
            remote(piece, piece, ssend.at[b, j], srecv.at[b, j], right).wait_send()
        for k in range(4):
            piece = gath.at[b, x] if k < 2 else gath.at[b, x, :, lo]
            remote(piece, piece, gsend.at[b, k], grecv.at[b, k], right).wait_send()
        return 0

    lax.fori_loop(0, nb, sent, 0)
    for w in range(3):
        weight_sent(w)


def shards(
    tokens, spatial_modulation, spatial_weights_in, spatial_weights_out,
    temporal_modulation, temporal_weights_in, temporal_weights_out,
):
    d = tokens.shape[-1]
    nb = BLOCKS
    hb = d // 2
    dma = pltpu.SemaphoreType.DMA
    any_space = pl.BlockSpec(memory_space=pl.ANY)
    vmem = pl.BlockSpec(memory_space=pltpu.VMEM)
    out_weights = pltpu.VMEM((4, 4, 2, 16, d), BF)
    ring = [
        pltpu.VMEM((nb, 4, 16, d), BF),
        pltpu.VMEM((nb, 2, 16, hb), BF),
        pltpu.VMEM((nb, 2, 2, 16, hb), BF),
    ]
    result = pl.pallas_call(
        kernel,
        out_shape=jax.ShapeDtypeStruct((80, d), BF),
        in_specs=[any_space, vmem, any_space, any_space, vmem, any_space, any_space],
        out_specs=any_space,
        scratch_shapes=[
            pltpu.VMEM((4, 320, d), BF),
            pltpu.VMEM((d, 384), BF),
            pltpu.VMEM((d, 512), BF),
            pltpu.VMEM((1280, 128), BF),
            pltpu.VMEM((1280, 128), BF),
            pltpu.VMEM((1280, 256), BF),
            pltpu.VMEM((nb, 4, 64, 128), BF),
            pltpu.VMEM((nb, 4, 64, 128), BF),
            pltpu.VMEM((80, d), BF),
            out_weights,
            pltpu.VMEM((4, 4, 4, d // 16, 384), BF),
            out_weights,
            *ring,
            pltpu.VMEM((nb, 8, 16, d // 8), BF),
            pltpu.VMEM((nb, 8, 16, d // 8), BF),
            pltpu.VMEM((nb, 4, 16, d), BF),
            *ring,
            pltpu.VMEM((nb, 16, d), BF),
            dma((3,)), dma((4,)), dma((nb,)), dma(()),
            dma((3, 9, 4)), dma((3, 9, 4)),
            dma((nb, 4)), dma((nb, 4)),
            dma((nb, 6)), dma((nb, 6)),
            dma((nb, 8)), dma((nb, 8)),
            dma((nb, 4)), dma((nb, 4)),
            dma((nb, 6)), dma((nb, 6)),
        ],
        compiler_params=pltpu.CompilerParams(
            collective_id=0, has_side_effects=True, vmem_limit_bytes=60 * 1024 * 1024
        ),
        cost_estimate=pl.CostEstimate(
            flops=9_000_000_000, bytes_accessed=16_000_000, transcendentals=2_000_000
        ),
    )(
        tokens.reshape(4, 320, d),
        spatial_modulation,
        jnp.transpose(spatial_weights_in, (1, 0, 2)).reshape(d, 384),
        spatial_weights_out.reshape(4, 2, 16, d),
        temporal_modulation,
        jnp.transpose(temporal_weights_in, (1, 0, 2)).reshape(4, 4, d // 16, 384),
        temporal_weights_out.reshape(4, 2, 16, d),
    )
    return jnp.transpose(result.reshape(10, 8, d), (1, 0, 2))


def solution(mesh):
    placed = (
        P("seq", None, None),
        P(),
        P(None, "head", None),
        P("head", None, None),
        P(),
        P(None, "head", None),
        P("head", None, None),
    )
    return jax.shard_map(
        shards,
        mesh=mesh,
        in_specs=placed,
        out_specs=P(None, ("seq", "head"), None),
        check_vma=False,
    )
```

```python
import functools

import jax
import jax.numpy as jnp
from jax import lax
from jax.experimental import pallas as pl
from jax.experimental.pallas import tpu as pltpu
from jax.sharding import PartitionSpec as P

BF = jnp.bfloat16
F32 = jnp.float32
MESH = pl.DeviceIdType.MESH
BLOCKS = 5
LOG2E = 1.4426950408889634
TABLE = (
    ("attend", (0, 0), (1, 1), (2, 2), (4, 3), (5, 4)),
    ("rest", 2, 0),
    ("sum_begin", (2, 0), (3, 1), (4, 2), (7, 3), (8, 4)),
    ("sum_second", (5, 0), (6, 1), (7, 2), (9, 3), (10, 4)),
    ("swap_send", (7, 0), (8, 1), (10, 2), (11, 3), (12, 4)),
    ("gather_send", (9, 0), (10, 1), (11, 2), (12, 3), (14, 4)),
    ("gather_relay", (11, 0), (12, 1), (13, 2), (14, 3), (15, 4)),
    ("rest", 12, 1),
    ("rest", 14, 2),
    ("temporal", 14, 0, 2),
    ("temporal", 15, 2, 4),
    ("temporal", 17, 4, 5),
    ("back_second", (15, 0), (16, 1), (17, 2), (18, 3), (19, 4)),
    ("finish", (17, 0), (18, 1), (19, 2), (20, 3), (21, 4)),
    ("quarter", 0, 1, 0),
    ("quarter", 4, 1, 1),
    ("quarter", 5, 1, 2),
    ("quarter", 8, 1, 3),
    ("quarter", 11, 2, 0),
    ("quarter", 12, 2, 1),
    ("half", 4, 1),
    ("half", 11, 2),
)
COUNT = 22
CROSS = ((0, 0), (0, 1), (0, -1), (1, 0), (1, 1), (1, -1), (1, 2), (1, 3), (2, 0), (2, 1), (2, -1))


def dot(a, b):
    return jnp.dot(a, b, preferred_element_type=F32)


def dot_nt(a, b):
    return lax.dot_general(a, b, (((1,), (1,)), ((), ())), preferred_element_type=F32)


def iota(shape, axis):
    return lax.broadcasted_iota(jnp.int32, shape, axis)


def one_hot(hit):
    return jnp.where(hit, 1.0, 0.0).astype(BF)


def remote(src, dst, send, recv, device):
    return pltpu.make_async_remote_copy(
        src_ref=src, dst_ref=dst, send_sem=send, recv_sem=recv,
        device_id=device, device_id_type=MESH,
    )


def kernel(
    tok_in, smod, win_in, wo_in, tmod, wt_in, wto_in,
    out,
    tok, wi, wx, qb, kb, vx, att, cat, own_rows, wo, wt, wto,
    part, relay, got, shuf, shufr, gath, part2, relay2, got2, res,
    local_sem, tok_sem, out_sem, win_sem, wsend, wrecv, asend, arecv,
    rsend, rrecv, ssend, srecv, gsend, grecv, rsend2, rrecv2,
):
    d = tok.shape[-1]
    nb = BLOCKS
    hb = d // 2
    eighth = d // 8
    s = lax.axis_index("seq")
    h = lax.axis_index("head")
    yl, z = s // 4, s % 4
    x, q = h // 4, h % 4
    yh, core = q // 2, q % 2
    right = (s, ((x + 1) % 4) * 4 + q)
    left = (s, ((x + 3) % 4) * 4 + q)
    quarters = [((yh + r // 2) % 2) * 2 + (core + r) % 2 for r in range(4)]
    quad = [(s, x * 4 + k) for k in quarters]
    mate = quad[1]
    cross = ((1 - yl) * 4 + z, x * 4 + (1 - yh) * 2 + core)
    beside = ((1 - yl) * 4 + z, h)
    up = (yl * 4 + (z + 1) % 4, h)
    down = (yl * 4 + (z + 3) % 4, h)
    xr, xl, xo = (x + 1) % 4, (x + 3) % 4, (x + 2) % 4
    zu, zd, zo = (z + 1) % 4, (z + 3) % 4, (z + 2) % 4

    barrier = pltpu.get_barrier_semaphore()
    partners = [right, left] + quad[1:] + [cross] + [((s + j) % 8, h) for j in range(1, 8)]
    for device in partners:
        pl.semaphore_signal(barrier, inc=1, device_id=device, device_id_type=MESH)

    load_w = pltpu.make_async_copy(win_in, wi, win_sem)
    load_w.start()
    for i in range(4):
        pltpu.make_async_copy(tok_in.at[i], tok.at[i], tok_sem.at[i]).start()
    weights = ((wo_in, wo), (wt_in, wt), (wto_in, wto))
    own_loads = [
        pltpu.make_async_copy(wo_in, wo.at[0], local_sem.at[0]),
        pltpu.make_async_copy(wt_in, wt.at[:, :, :, pl.ds(0, 384)], local_sem.at[1]),
        pltpu.make_async_copy(wto_in, wto.at[0], local_sem.at[2]),
    ]
    for load in own_loads:
        load.start()

    counts = (2, 4, 2)

    def at(w, slot, *where):
        buf = weights[w][1]
        if w == 1:
            where = where + (slice(None),) * (3 - len(where))
            return buf.at[where + (pl.ds(slot * 384, 384),)]
        return buf.at[(slot,) + where]

    def copy_of(w, kind, k, piece, to, device):
        return remote(piece, to, wsend.at[w, kind, k], wrecv.at[w, kind, k], device)

    def halves(w):
        m = counts[w] // 2
        return pl.ds(yl * m, m), pl.ds((1 - yl) * m, m)

    def weight_near(w):
        copy_of(w, 0, 0, weights[w][0], at(w, 1), mate).start()

    def weight_cross(w, k):
        copy_of(w, 1, k, weights[w][0].at[z, k], at(w, 2, z, k), cross).start()

    def weight_cross_half(w):
        theirs = halves(w)[1]
        copy_of(w, 2, 0, weights[w][0].at[zo, theirs], at(w, 2, zo, theirs), cross).start()

    def weight_quarter(w, k):
        piece = at(w, 2, z, k)
        copy_of(w, 1, k, piece, piece, cross).wait_recv()
        copy_of(w, 3, k, piece, piece, up).start()
        copy_of(w, 4, k, piece, piece, down).start()
        copy_of(w, 5, k, piece, at(w, 3, z, k), mate).start()

    def weight_half(w):
        mine = halves(w)[0]
        piece = at(w, 2, zo, mine)
        copy_of(w, 2, 0, piece, piece, cross).wait_recv()
        copy_of(w, 6, 0, piece, piece, beside).start()
        copy_of(w, 7, 0, piece, at(w, 3, zo, mine), mate).start()

    def weight_rest(w):
        for kind, zz in ((3, zd), (4, zu)):
            for k in range(counts[w]):
                piece = at(w, 2, zz, k)
                copy_of(w, kind, k, piece, piece, up).wait_recv()
            copy_of(w, 8, kind - 3, at(w, 2, zz), at(w, 3, zz), mate).start()
        theirs = halves(w)[1]
        piece = at(w, 2, zo, theirs)
        copy_of(w, 6, 0, piece, piece, beside).wait_recv()
        copy_of(w, 8, 2, piece, at(w, 3, zo, theirs), mate).start()

    def weight_end(w):
        mine, theirs = halves(w)
        own_loads[w].wait()
        copy_of(w, 0, 0, weights[w][0], at(w, 1), mate).wait_recv()
        for k in range(counts[w]):
            copy_of(w, 5, k, at(w, 3, z, k), at(w, 3, z, k), mate).wait_recv()
        copy_of(w, 7, 0, at(w, 3, zo, mine), at(w, 3, zo, mine), mate).wait_recv()
        for k, zz in ((0, zd), (1, zu)):
            copy_of(w, 8, k, at(w, 3, zz), at(w, 3, zz), mate).wait_recv()
        copy_of(w, 8, 2, at(w, 3, zo, theirs), at(w, 3, zo, theirs), mate).wait_recv()

    def weight_sent(w):
        piece, half, whole = at(w, 2, z, 0), at(w, 2, zo, halves(w)[0]), at(w, 2, z)
        copy_of(w, 0, 0, weights[w][0], at(w, 1), mate).wait_send()
        for kind, device in ((1, cross), (3, up), (4, down), (5, mate)):
            for k in range(counts[w]):
                copy_of(w, kind, k, piece, piece, device).wait_send()
        for kind, device in ((2, cross), (6, beside), (7, mate)):
            copy_of(w, kind, 0, half, half, device).wait_send()
        for k in range(2):
            copy_of(w, 8, k, whole, whole, mate).wait_send()
        copy_of(w, 8, 2, half, half, mate).wait_send()

    pl.semaphore_wait(barrier, len(partners))
    for w, k in CROSS:
        if k < 0:
            weight_cross_half(w)
        else:
            weight_cross(w, k)
    for w in range(3):
        weight_near(w)

    load_w.wait()
    m0 = smod[0:1, :]
    m0_high = m0.astype(BF).astype(F32)
    row = iota((16, d), 0)
    shift_rows = jnp.where(row == 0, m0_high, jnp.where(row == 1, m0 - m0_high, 0.0)).astype(BF)
    bias = jnp.sum(dot(shift_rows, wi[...]), axis=0, keepdims=True)

    def fold(i, _):
        rows = pl.ds(pl.multiple_of(i * 128, 128), 128)
        gain = jnp.broadcast_to(1.0 + smod[1:2, rows], (128, 128)).T
        for j in range(3):
            cols = slice(j * 128, (j + 1) * 128)
            wx[rows, cols] = (wi[rows, cols].astype(F32) * gain).astype(BF)
        wx[rows, 384:512] = jnp.ones((128, 128), BF)
        return 0

    lax.fori_loop(0, d // 128, fold, 0, unroll=4)
    colsum = dot(jnp.ones((16, d), BF), wx[:, 0:384])[0:1, :]

    def project(i, _):
        pltpu.make_async_copy(tok_in.at[i], tok.at[i], tok_sem.at[i]).wait()

        @pl.when(i == 3)
        def _():
            weight_quarter(0, 0)
            weight_quarter(0, 1)
            weight_half(0)

        t = tok[i]
        raw = dot(t, wx[...])
        base = t[:, 0:1].astype(F32)
        squares = jnp.zeros((320, 128), F32)
        for j in range(d // 128):
            e = t[:, j * 128:(j + 1) * 128].astype(F32) - base
            squares = squares + e * e
        mean = raw[:, 384:385] * (1.0 / d)
        spread = jnp.sum(squares, axis=1, keepdims=True) * (1.0 / d) - (mean - base) * (mean - base)
        scale = lax.rsqrt(spread + 1e-06)
        full = ((raw[:, 0:384] - mean * colsum) * scale + bias).astype(BF)
        rows = pl.ds(pl.multiple_of(i * 320, 320), 320)
        qb[rows, :] = full[:, 0:128]
        kb[rows, :] = full[:, 128:256]
        vx[rows, 0:128] = full[:, 256:384]
        vx[rows, 128:256] = jnp.ones((320, 128), BF)
        return 0

    lax.fori_loop(0, 4, project, 0)

    score_scale = 128 ** (-0.5) * LOG2E

    r256 = iota((256, 1), 0)
    spot = ((r256 >> 1) & 7) * 160 + ((r256 >> 4) & 3) * 40 + (r256 >> 6) * 10 + (r256 & 1)
    cells = iota((1, 1280), 1)

    def attend(b):
        queries = dot(one_hot(spot + 2 * b == cells), qb[...]).astype(BF)
        scores = dot_nt(queries, kb[...])
        top = jnp.max(scores, axis=1, keepdims=True)
        probs = jnp.exp2((scores - top) * score_scale).astype(BF)
        both = dot(probs, vx[...])
        att[b] = (both[:, 0:128] / both[:, 128:256]).astype(BF).reshape(4, 64, 128)
        for r in (2, 3, 1):
            remote(att.at[b, quarters[r]], cat.at[b, r], asend.at[b, r], arecv.at[b, r], quad[r]).start()


    first = h * 10
    start = jnp.minimum((first // 16) * 16, 128)
    skip = first - start
    r80 = iota((80, 1), 0)
    target = ((r80 >> 1) & 7) * 32 + (r80 >> 4) * 2 + (r80 & 1) + skip
    flat = tok.reshape(1280, d)
    windows = jnp.concatenate(
        [flat[pl.ds(pl.multiple_of(k * 160 + start, 16), 32), :] for k in range(8)], axis=0
    )
    own_rows[...] = dot(one_hot(target == iota((1, 256), 1)), windows).astype(BF)

    r128 = iota((128, 1), 0)
    c128 = iota((1, 128), 1)
    to_send = one_hot((r128 & 7) * 16 + (r128 >> 4) * 2 + ((r128 >> 3) & 1) == c128)
    from_recv = one_hot((r128 & 7) * 16 + ((r128 >> 3) & 1) * 8 + (r128 >> 4) == c128)
    lo, hi = pl.ds(0, hb), pl.ds(hb, hb)

    def ring_first(b, buf, rel, rec, ss, rs):
        remote(buf.at[b, xo, :, lo], rel.at[b, 0], ss.at[b, 0], rs.at[b, 0], right).start()
        remote(buf.at[b, xo, :, hi], rel.at[b, 1], ss.at[b, 1], rs.at[b, 1], left).start()
        remote(buf.at[b, xr, :, hi], rec.at[b, 0, 1], ss.at[b, 2], rs.at[b, 2], right).start()
        remote(buf.at[b, xl, :, lo], rec.at[b, 1, 0], ss.at[b, 3], rs.at[b, 3], left).start()

    def ring_second(b, buf, rel, rec, ss, rs):
        remote(rel.at[b, 0], rel.at[b, 0], ss.at[b, 0], rs.at[b, 0], right).wait_recv()
        rel[b, 0] = (rel[b, 0].astype(F32) + buf[b, xr, :, lo].astype(F32)).astype(BF)
        remote(rel.at[b, 0], rec.at[b, 0, 0], ss.at[b, 4], rs.at[b, 4], right).start()
        remote(rel.at[b, 1], rel.at[b, 1], ss.at[b, 1], rs.at[b, 1], left).wait_recv()
        rel[b, 1] = (rel[b, 1].astype(F32) + buf[b, xl, :, hi].astype(F32)).astype(BF)
        remote(rel.at[b, 1], rec.at[b, 1, 1], ss.at[b, 5], rs.at[b, 5], left).start()

    def ring_last(b, buf, rec, ss, rs):
        for k, side, half in ((2, 0, 1), (3, 1, 0), (4, 0, 0), (5, 1, 1)):
            piece = rec.at[b, side, half]
            remote(piece, piece, ss.at[b, k], rs.at[b, k], right).wait_recv()
        own = buf[b, x].astype(F32)
        halves = [
            own[:, k * hb:(k + 1) * hb] + rec[b, 0, k].astype(F32) + rec[b, 1, k].astype(F32)
            for k in range(2)
        ]
        return jnp.concatenate(halves, axis=1)

    def ring_sent(b, rel, ss, rs):
        for k in range(6):
            remote(rel.at[b, 0], rel.at[b, 0], ss.at[b, k], rs.at[b, k], right).wait_send()

    def sum_begin(b):
        @pl.when(b == 0)
        def _():
            weight_end(0)

        for r in (1, 2, 3):
            remote(cat.at[b, r], cat.at[b, r], asend.at[b, r], arecv.at[b, r], quad[r]).wait_recv()
        lhs = jnp.concatenate([att[b, q], cat[b, 1], cat[b, 2], cat[b, 3]], axis=1)
        part[b] = dot(lhs, wo[...].reshape(512, d)).astype(BF).reshape(4, 16, d)
        ring_first(b, part, relay, got, rsend, rrecv)

    def swap_send(b):
        total = ring_last(b, part, got, rsend, rrecv)
        rows = own_rows[pl.ds(pl.multiple_of(b * 16, 16), 16), :]
        middle = (rows.astype(F32) + smod[2:3, :] * total).astype(BF)
        stacked = jnp.concatenate([middle[:, k * eighth:(k + 1) * eighth] for k in range(8)], axis=0)
        shuf[b] = dot(to_send, stacked).astype(BF).reshape(8, 16, eighth)
        for j in (4, 1, 7, 5, 3, 2, 6):
            to = (s + j) % 8
            remote(shuf.at[b, to], shufr.at[b, s], ssend.at[b, j], srecv.at[b, j], (to, h)).start()
        shufr[b, s] = shuf[b, s]

    def gather_send(b):
        for j in range(1, 8):
            piece = shufr.at[b, (s + 8 - j) % 8]
            remote(piece, piece, ssend.at[b, j], srecv.at[b, j], right).wait_recv()
        rows = dot(from_recv, shufr[b].reshape(128, eighth)).astype(BF)
        gath[b, x] = jnp.concatenate([rows[k * 16:(k + 1) * 16, :] for k in range(8)], axis=1)
        mine = gath.at[b, x]
        remote(mine, mine, gsend.at[b, 0], grecv.at[b, 0], right).start()
        remote(mine, mine, gsend.at[b, 1], grecv.at[b, 1], left).start()

    def gather_relay(b):
        from_left, from_right = gath.at[b, xl], gath.at[b, xr]
        remote(from_left, from_left, gsend.at[b, 0], grecv.at[b, 0], right).wait_recv()
        piece = gath.at[b, xl, :, lo]
        remote(piece, piece, gsend.at[b, 2], grecv.at[b, 2], right).start()
        remote(from_right, from_right, gsend.at[b, 1], grecv.at[b, 1], left).wait_recv()
        piece = gath.at[b, xr, :, hi]
        remote(piece, piece, gsend.at[b, 3], grecv.at[b, 3], left).start()

    def temporal(lead, last):
        n = (last - lead) * 64
        for b in range(lead, last):
            far = gath.at[b, xo]
            remote(far.at[:, lo], far.at[:, lo], gsend.at[b, 2], grecv.at[b, 2], right).wait_recv()
            remote(far.at[:, hi], far.at[:, hi], gsend.at[b, 3], grecv.at[b, 3], left).wait_recv()
        rows = gath[lead:last].reshape(n, d).astype(F32)
        center = rows - jnp.sum(rows, axis=1, keepdims=True) * (1.0 / d)
        spread = jnp.sum(center * center, axis=1, keepdims=True) * (1.0 / d)
        scale = lax.rsqrt(spread + 1e-06)
        normed = (center * scale * (1.0 + tmod[1:2, :]) + tmod[0:1, :]).astype(BF)
        if lead == 0:
            weight_end(1)
        joined = dot(normed, wt[...].reshape(d, 1536)).astype(BF)
        same = (iota((n, n), 0) >> 3) == (iota((n, n), 1) >> 3)
        attended = []
        for j in range(4):
            mine = joined[:, j * 384:(j + 1) * 384]
            scores = jnp.where(same, dot_nt(mine[:, 0:128], mine[:, 128:256]), -1e30)
            top = jnp.max(scores, axis=1, keepdims=True)
            probs = jnp.exp2((scores - top) * score_scale)
            probs = (probs / jnp.sum(probs, axis=1, keepdims=True)).astype(BF)
            attended.append(dot(probs, mine[:, 256:384]).astype(BF))
        if lead == 0:
            weight_end(2)
        lhs = jnp.concatenate(attended, axis=1)
        part2[lead:last] = dot(lhs, wto[...].reshape(512, d)).astype(BF).reshape(last - lead, 4, 16, d)
        for b in range(lead, last):
            ring_first(b, part2, relay2, got2, rsend2, rrecv2)

    def back_second(b):
        ring_second(b, part2, relay2, got2, rsend2, rrecv2)

    def finish(b):
        total = ring_last(b, part2, got2, rsend2, rrecv2)
        res[b] = (gath[b, x].astype(F32) + tmod[2:3, :] * total).astype(BF)
        rows = pl.ds(pl.multiple_of(b * 16, 16), 16)
        pltpu.make_async_copy(res.at[b], out.at[rows, :], out_sem.at[b]).start()

    def sum_second(b):
        ring_second(b, part, relay, got, rsend, rrecv)

    blocks = {
        "attend": attend, "sum_begin": sum_begin, "sum_second": sum_second, "swap_send": swap_send,
        "gather_send": gather_send, "gather_relay": gather_relay, "back_second": back_second, "finish": finish,
    }
    moves = {"temporal": temporal, "quarter": weight_quarter, "half": weight_half, "rest": weight_rest}

    def tick(t, _):
        for name, *what in TABLE:
            if name in blocks:
                hit, b = t < 0, 0
                for when, block in what:
                    hit = hit | (t == when)
                    b = b + jnp.where(t == when, block, 0)

                @pl.when(hit)
                def _(name=name, b=b):
                    blocks[name](b)
            else:
                @pl.when(t == what[0])
                def _(name=name, what=what):
                    moves[name](*what[1:])

        return 0

    lax.fori_loop(0, COUNT, tick, 0)

    for b in range(nb):
        pltpu.make_async_copy(res.at[b], out.at[pl.ds(b * 16, 16), :], out_sem.at[b]).wait()

    def sent(b, _):
        for r in (1, 2, 3):
            remote(cat.at[b, r], cat.at[b, r], asend.at[b, r], arecv.at[b, r], quad[r]).wait_send()
        ring_sent(b, relay, rsend, rrecv)
        ring_sent(b, relay2, rsend2, rrecv2)
        for j in range(1, 8):
            piece = shuf.at[b, 0]
            remote(piece, piece, ssend.at[b, j], srecv.at[b, j], right).wait_send()
        for k in range(4):
            piece = gath.at[b, x] if k < 2 else gath.at[b, x, :, lo]
            remote(piece, piece, gsend.at[b, k], grecv.at[b, k], right).wait_send()
        return 0

    lax.fori_loop(0, nb, sent, 0)
    for w in range(3):
        weight_sent(w)


def shards(
    tokens, spatial_modulation, spatial_weights_in, spatial_weights_out,
    temporal_modulation, temporal_weights_in, temporal_weights_out,
):
    d = tokens.shape[-1]
    nb = BLOCKS
    hb = d // 2
    dma = pltpu.SemaphoreType.DMA
    any_space = pl.BlockSpec(memory_space=pl.ANY)
    vmem = pl.BlockSpec(memory_space=pltpu.VMEM)
    out_weights = pltpu.VMEM((4, 4, 2, 16, d), BF)
    ring = [
        pltpu.VMEM((nb, 4, 16, d), BF),
        pltpu.VMEM((nb, 2, 16, hb), BF),
        pltpu.VMEM((nb, 2, 2, 16, hb), BF),
    ]
    result = pl.pallas_call(
        kernel,
        out_shape=jax.ShapeDtypeStruct((80, d), BF),
        in_specs=[any_space, vmem, any_space, any_space, vmem, any_space, any_space],
        out_specs=any_space,
        scratch_shapes=[
            pltpu.VMEM((4, 320, d), BF),
            pltpu.VMEM((d, 384), BF),
            pltpu.VMEM((d, 512), BF),
            pltpu.VMEM((1280, 128), BF),
            pltpu.VMEM((1280, 128), BF),
            pltpu.VMEM((1280, 256), BF),
            pltpu.VMEM((nb, 4, 64, 128), BF),
            pltpu.VMEM((nb, 4, 64, 128), BF),
            pltpu.VMEM((80, d), BF),
            out_weights,
            pltpu.VMEM((4, 4, d // 16, 1536), BF),
            out_weights,
            *ring,
            pltpu.VMEM((nb, 8, 16, d // 8), BF),
            pltpu.VMEM((nb, 8, 16, d // 8), BF),
            pltpu.VMEM((nb, 4, 16, d), BF),
            *ring,
            pltpu.VMEM((nb, 16, d), BF),
            dma((3,)), dma((4,)), dma((nb,)), dma(()),
            dma((3, 9, 4)), dma((3, 9, 4)),
            dma((nb, 4)), dma((nb, 4)),
            dma((nb, 6)), dma((nb, 6)),
            dma((nb, 8)), dma((nb, 8)),
            dma((nb, 4)), dma((nb, 4)),
            dma((nb, 6)), dma((nb, 6)),
        ],
        compiler_params=pltpu.CompilerParams(
            collective_id=0, has_side_effects=True, vmem_limit_bytes=60 * 1024 * 1024
        ),
        cost_estimate=pl.CostEstimate(
            flops=9_000_000_000, bytes_accessed=16_000_000, transcendentals=2_000_000
        ),
    )(
        tokens.reshape(4, 320, d),
        spatial_modulation,
        jnp.transpose(spatial_weights_in, (1, 0, 2)).reshape(d, 384),
        spatial_weights_out.reshape(4, 2, 16, d),
        temporal_modulation,
        jnp.transpose(temporal_weights_in, (1, 0, 2)).reshape(4, 4, d // 16, 384),
        temporal_weights_out.reshape(4, 2, 16, d),
    )
    return jnp.transpose(result.reshape(10, 8, d), (1, 0, 2))


def solution(mesh):
    placed = (
        P("seq", None, None),
        P(),
        P(None, "head", None),
        P("head", None, None),
        P(),
        P(None, "head", None),
        P("head", None, None),
    )
    return jax.shard_map(
        shards,
        mesh=mesh,
        in_specs=placed,
        out_specs=P(None, ("seq", "head"), None),
        check_vma=False,
    )
```

```python
import functools

import jax
import jax.numpy as jnp
from jax import lax
from jax.experimental import pallas as pl
from jax.experimental.pallas import tpu as pltpu
from jax.sharding import PartitionSpec as P

BF = jnp.bfloat16
F32 = jnp.float32
MESH = pl.DeviceIdType.MESH
BLOCKS = 5
LOG2E = 1.4426950408889634
TABLE = (
    ("attend", (0, 0), (1, 1), (2, 2), (5, 3), (6, 4)),
    ("rest", 1, 0),
    ("sum_begin", (3, 0), (4, 1), (5, 2), (7, 3), (8, 4)),
    ("sum_second", (5, 0), (6, 1), (7, 2), (8, 3), (10, 4)),
    ("swap_send", (7, 0), (8, 1), (9, 2), (10, 3), (12, 4)),
    ("gather_send", (9, 0), (10, 1), (11, 2), (12, 3), (14, 4)),
    ("gather_relay", (11, 0), (12, 1), (13, 2), (14, 3), (15, 4)),
    ("rest", 13, 1),
    ("rest", 13, 2),
    ("temporal", 14, 0, 2),
    ("temporal", 15, 2, 4),
    ("temporal", 17, 4, 5),
    ("back_second", (15, 0), (16, 1), (17, 2), (18, 3), (19, 4)),
    ("finish", (17, 0), (18, 1), (19, 2), (20, 3), (21, 4)),
    ("quarter", 0, 1, 0),
    ("quarter", 2, 1, 1),
    ("quarter", 4, 1, 2),
    ("quarter", 5, 1, 3),
    ("quarter", 6, 2, 0),
    ("quarter", 7, 2, 1),
    ("relay", 9, 1, 0),
    ("relay", 10, 1, 1),
    ("relay", 12, 2, 0),
)
COUNT = 22


def dot(a, b):
    return jnp.dot(a, b, preferred_element_type=F32)


def dot_nt(a, b):
    return lax.dot_general(a, b, (((1,), (1,)), ((), ())), preferred_element_type=F32)


def iota(shape, axis):
    return lax.broadcasted_iota(jnp.int32, shape, axis)


def one_hot(hit):
    return jnp.where(hit, 1.0, 0.0).astype(BF)


def remote(src, dst, send, recv, device):
    return pltpu.make_async_remote_copy(
        src_ref=src, dst_ref=dst, send_sem=send, recv_sem=recv,
        device_id=device, device_id_type=MESH,
    )


def kernel(
    tok_in, smod, win_in, wo_in, tmod, wt_in, wto_in,
    out,
    tok, shift, wi, wx, qb, kb, vx, att, cat, own_rows, wo, wt, wto,
    part, relay, got, shuf, shufr, gath, part2, relay2, got2, res,
    local_sem, tok_sem, out_sem, win_sem, wsend, wrecv, asend, arecv,
    rsend, rrecv, ssend, srecv, gsend, grecv, rsend2, rrecv2,
):
    d = tok.shape[-1]
    nb = BLOCKS
    hb = d // 2
    eighth = d // 8
    s = lax.axis_index("seq")
    h = lax.axis_index("head")
    yl, z = s // 4, s % 4
    x, q = h // 4, h % 4
    yh, core = q // 2, q % 2
    right = (s, ((x + 1) % 4) * 4 + q)
    left = (s, ((x + 3) % 4) * 4 + q)
    quarters = [((yh + r // 2) % 2) * 2 + (core + r) % 2 for r in range(4)]
    quad = [(s, x * 4 + k) for k in quarters]
    mate = quad[1]
    cross = ((1 - yl) * 4 + z, x * 4 + (1 - yh) * 2 + core)
    beside = ((1 - yl) * 4 + z, h)
    up = (yl * 4 + (z + 1) % 4, h)
    down = (yl * 4 + (z + 3) % 4, h)
    xr, xl, xo = (x + 1) % 4, (x + 3) % 4, (x + 2) % 4
    zu, zd, zo = (z + 1) % 4, (z + 3) % 4, (z + 2) % 4

    barrier = pltpu.get_barrier_semaphore()
    partners = [right, left] + quad[1:] + [cross] + [((s + j) % 8, h) for j in range(1, 8)]
    for device in partners:
        pl.semaphore_signal(barrier, inc=1, device_id=device, device_id_type=MESH)

    load_w = pltpu.make_async_copy(win_in, wi, win_sem)
    load_w.start()
    for i in range(4):
        pltpu.make_async_copy(tok_in.at[i], tok.at[i, pl.ds(0, 320)], tok_sem.at[i]).start()
    weights = ((wo_in, wo), (wt_in, wt), (wto_in, wto))
    own_loads = [
        pltpu.make_async_copy(wo_in, wo.at[0], local_sem.at[0]),
        pltpu.make_async_copy(wt_in, wt.at[:, :, :, pl.ds(0, 384)], local_sem.at[1]),
        pltpu.make_async_copy(wto_in, wto.at[0], local_sem.at[2]),
    ]
    for load in own_loads:
        load.start()

    counts = (2, 4, 2)

    def at(w, slot, *where):
        buf = weights[w][1]
        if w == 1:
            where = where + (slice(None),) * (3 - len(where))
            return buf.at[where + (pl.ds(slot * 384, 384),)]
        return buf.at[(slot,) + where]

    def copy_of(w, kind, k, piece, to, device):
        return remote(piece, to, wsend.at[w, kind, k], wrecv.at[w, kind, k], device)

    def first_quarter(step):
        return (z + 2 * yl + step) % 4

    def weight_near(w):
        copy_of(w, 0, 0, weights[w][0], at(w, 1), mate).start()

    def weight_cross(w):
        for k in range(counts[w]):
            quarter = z if w else first_quarter(2)
            copy_of(w, 1, k, weights[w][0].at[quarter, k], at(w, 2, quarter, k), cross).start()

    def weight_quarter(w, k):
        quarter = z if w else first_quarter(0)
        piece = at(w, 2, quarter, k)
        copy_of(w, 1, k, piece, piece, cross).wait_recv()
        copy_of(w, 3, k, piece, piece, up).start()
        copy_of(w, 4, k, piece, piece, down).start()
        if w == 0:
            copy_of(w, 6, k, piece, piece, beside).start()
        copy_of(w, 5, k, piece, at(w, 3, quarter, k), mate).start()

    def weight_relay(w, k):
        m = counts[w] // 2
        below, above = at(w, 2, zd, k), at(w, 2, zu, m + k)
        copy_of(w, 3, k, below, below, up).wait_recv()
        copy_of(w, 6, k, below, below, up).start()
        copy_of(w, 4, m + k, above, above, down).wait_recv()
        copy_of(w, 7, k, above, above, down).start()

    def weight_rest(w):
        if w == 0:
            for j, kind, step in ((0, 3, 3), (1, 4, 1), (2, 6, 2)):
                quarter = first_quarter(step)
                for k in range(counts[w]):
                    piece = at(w, 2, quarter, k)
                    copy_of(w, kind, k, piece, piece, up).wait_recv()
                copy_of(w, 8, j, at(w, 2, quarter), at(w, 3, quarter), mate).start()
            return
        m = counts[w] // 2
        for k in range(m, 2 * m):
            piece = at(w, 2, zd, k)
            copy_of(w, 3, k, piece, piece, up).wait_recv()
        copy_of(w, 8, 0, at(w, 2, zd), at(w, 3, zd), mate).start()
        for k in range(m):
            piece = at(w, 2, zu, k)
            copy_of(w, 4, k, piece, piece, down).wait_recv()
        copy_of(w, 8, 1, at(w, 2, zu), at(w, 3, zu), mate).start()
        for k in range(m):
            piece = at(w, 2, zo, k)
            copy_of(w, 6, k, piece, piece, up).wait_recv()
            piece = at(w, 2, zo, m + k)
            copy_of(w, 7, k, piece, piece, down).wait_recv()
        copy_of(w, 8, 2, at(w, 2, zo), at(w, 3, zo), mate).start()

    def weight_end(w):
        own_loads[w].wait()
        copy_of(w, 0, 0, weights[w][0], at(w, 1), mate).wait_recv()
        near, rest = (z, (zd, zu, zo)) if w else (first_quarter(0), [first_quarter(k) for k in (3, 1, 2)])
        for k in range(counts[w]):
            copy_of(w, 5, k, at(w, 3, near, k), at(w, 3, near, k), mate).wait_recv()
        for k, quarter in enumerate(rest):
            copy_of(w, 8, k, at(w, 3, quarter), at(w, 3, quarter), mate).wait_recv()

    def weight_sent(w):
        piece, whole = at(w, 2, z, 0), at(w, 2, z)
        copy_of(w, 0, 0, weights[w][0], at(w, 1), mate).wait_send()
        for kind in (1, 3, 4, 5):
            for k in range(counts[w]):
                copy_of(w, kind, k, piece, piece, up).wait_send()
        for k in range(2 if w == 0 else counts[w] // 2):
            copy_of(w, 6, k, piece, piece, up).wait_send()
            if w:
                copy_of(w, 7, k, piece, piece, down).wait_send()
        for k in range(3):
            copy_of(w, 8, k, whole, whole, mate).wait_send()

    pl.semaphore_wait(barrier, len(partners))
    for w in range(3):
        weight_cross(w)
    for w in range(3):
        weight_near(w)

    load_w.wait()
    m0 = smod[0:1, :]
    m0_high = m0.astype(BF).astype(F32)
    row = iota((16, d), 0)
    shift_rows = jnp.where(row == 0, m0_high, jnp.where(row == 1, m0 - m0_high, 0.0)).astype(BF)
    shift[...] = shift_rows

    def fold(i, total):
        rows = pl.ds(pl.multiple_of(i * 128, 128), 128)
        gain = jnp.broadcast_to(1.0 + smod[1:2, rows], (128, 128)).T
        for j in range(3):
            cols = slice(j * 128, (j + 1) * 128)
            wx[rows, cols] = (wi[rows, cols].astype(F32) * gain).astype(BF)
        wx[rows, 384:512] = jnp.ones((128, 128), BF)
        return total + dot(shift[:, rows], wi[rows, :])

    bias = lax.fori_loop(0, d // 128, fold, jnp.zeros((16, 384), F32), unroll=4)
    bias = jnp.sum(bias, axis=0, keepdims=True)
    tok[:, 320:336] = jnp.ones((4, 16, d), BF)

    def project(i, _):
        pltpu.make_async_copy(tok_in.at[i], tok.at[i, pl.ds(0, 320)], tok_sem.at[i]).wait()

        @pl.when(i == 2)
        def _():
            weight_quarter(0, 0)

        @pl.when(i == 3)
        def _():
            weight_quarter(0, 1)

        every = dot(tok[i], wx[...])
        raw, colsum = every[0:320], every[320:321, 0:384]
        t = tok[i, 0:320]
        base = t[:, 0:1].astype(F32)
        squares = jnp.zeros((320, 128), F32)
        for j in range(d // 128):
            e = t[:, j * 128:(j + 1) * 128].astype(F32) - base
            squares = squares + e * e
        mean = raw[:, 384:385] * (1.0 / d)
        spread = jnp.sum(squares, axis=1, keepdims=True) * (1.0 / d) - (mean - base) * (mean - base)
        scale = lax.rsqrt(spread + 1e-06)
        full = ((raw[:, 0:384] - mean * colsum) * scale + bias).astype(BF)
        rows = pl.ds(pl.multiple_of(i * 320, 320), 320)
        qb[rows, :] = full[:, 0:128]
        kb[rows, :] = full[:, 128:256]
        vx[rows, 0:128] = full[:, 256:384]
        vx[rows, 128:256] = jnp.ones((320, 128), BF)
        return 0

    lax.fori_loop(0, 4, project, 0)

    score_scale = 128 ** (-0.5) * LOG2E

    r256 = iota((256, 1), 0)
    spot = ((r256 >> 1) & 7) * 160 + ((r256 >> 4) & 3) * 40 + (r256 >> 6) * 10 + (r256 & 1)
    cells = iota((1, 1280), 1)

    def attend(b):
        queries = dot(one_hot(spot + 2 * b == cells), qb[...]).astype(BF)
        scores = dot_nt(queries, kb[...])
        top = jnp.max(scores, axis=1, keepdims=True)
        probs = jnp.exp2((scores - top) * score_scale).astype(BF)
        both = dot(probs, vx[...])
        att[b] = (both[:, 0:128] / both[:, 128:256]).astype(BF).reshape(4, 64, 128)
        for r in (2, 3, 1):
            remote(att.at[b, quarters[r]], cat.at[b, r], asend.at[b, r], arecv.at[b, r], quad[r]).start()


    first = h * 10
    start = jnp.minimum((first // 16) * 16, 128)
    skip = first - start
    r80 = iota((80, 1), 0)
    target = ((r80 >> 1) & 7) * 32 + (r80 >> 4) * 2 + (r80 & 1) + skip
    windows = jnp.concatenate(
        [tok[k // 2, pl.ds(pl.multiple_of((k % 2) * 160 + start, 16), 32), :] for k in range(8)], axis=0
    )
    own_rows[...] = dot(one_hot(target == iota((1, 256), 1)), windows).astype(BF)

    r128 = iota((128, 1), 0)
    c128 = iota((1, 128), 1)
    to_send = one_hot((r128 & 7) * 16 + (r128 >> 4) * 2 + ((r128 >> 3) & 1) == c128)
    from_recv = one_hot((r128 & 7) * 16 + ((r128 >> 3) & 1) * 8 + (r128 >> 4) == c128)
    lo, hi = pl.ds(0, hb), pl.ds(hb, hb)

    def ring_first(b, buf, rel, rec, ss, rs):
        remote(buf.at[b, xo, :, lo], rel.at[b, 0], ss.at[b, 0], rs.at[b, 0], right).start()
        remote(buf.at[b, xo, :, hi], rel.at[b, 1], ss.at[b, 1], rs.at[b, 1], left).start()
        remote(buf.at[b, xr, :, hi], rec.at[b, 0, 1], ss.at[b, 2], rs.at[b, 2], right).start()
        remote(buf.at[b, xl, :, lo], rec.at[b, 1, 0], ss.at[b, 3], rs.at[b, 3], left).start()

    def ring_second(b, buf, rel, rec, ss, rs):
        remote(rel.at[b, 0], rel.at[b, 0], ss.at[b, 0], rs.at[b, 0], right).wait_recv()
        rel[b, 0] = (rel[b, 0].astype(F32) + buf[b, xr, :, lo].astype(F32)).astype(BF)
        remote(rel.at[b, 0], rec.at[b, 0, 0], ss.at[b, 4], rs.at[b, 4], right).start()
        remote(rel.at[b, 1], rel.at[b, 1], ss.at[b, 1], rs.at[b, 1], left).wait_recv()
        rel[b, 1] = (rel[b, 1].astype(F32) + buf[b, xl, :, hi].astype(F32)).astype(BF)
        remote(rel.at[b, 1], rec.at[b, 1, 1], ss.at[b, 5], rs.at[b, 5], left).start()

    def ring_last(b, buf, rec, ss, rs):
        for k, side, half in ((2, 0, 1), (3, 1, 0), (4, 0, 0), (5, 1, 1)):
            piece = rec.at[b, side, half]
            remote(piece, piece, ss.at[b, k], rs.at[b, k], right).wait_recv()
        own = buf[b, x].astype(F32)
        halves = [
            own[:, k * hb:(k + 1) * hb] + rec[b, 0, k].astype(F32) + rec[b, 1, k].astype(F32)
            for k in range(2)
        ]
        return jnp.concatenate(halves, axis=1)

    def ring_sent(b, rel, ss, rs):
        for k in range(6):
            remote(rel.at[b, 0], rel.at[b, 0], ss.at[b, k], rs.at[b, k], right).wait_send()

    def sum_begin(b):
        @pl.when(b == 0)
        def _():
            weight_end(0)

        for r in (1, 2, 3):
            remote(cat.at[b, r], cat.at[b, r], asend.at[b, r], arecv.at[b, r], quad[r]).wait_recv()
        lhs = jnp.concatenate([att[b, q], cat[b, 1], cat[b, 2], cat[b, 3]], axis=1)
        part[b] = dot(lhs, wo[...].reshape(512, d)).astype(BF).reshape(4, 16, d)
        ring_first(b, part, relay, got, rsend, rrecv)

    def swap_send(b):
        total = ring_last(b, part, got, rsend, rrecv)
        rows = own_rows[pl.ds(pl.multiple_of(b * 16, 16), 16), :]
        middle = (rows.astype(F32) + smod[2:3, :] * total).astype(BF)
        stacked = jnp.concatenate([middle[:, k * eighth:(k + 1) * eighth] for k in range(8)], axis=0)
        shuf[b] = dot(to_send, stacked).astype(BF).reshape(8, 16, eighth)
        for j in (4, 1, 7, 5, 3, 2, 6):
            to = (s + j) % 8
            remote(shuf.at[b, to], shufr.at[b, s], ssend.at[b, j], srecv.at[b, j], (to, h)).start()
        shufr[b, s] = shuf[b, s]

    def gather_send(b):
        for j in range(1, 8):
            piece = shufr.at[b, (s + 8 - j) % 8]
            remote(piece, piece, ssend.at[b, j], srecv.at[b, j], right).wait_recv()
        rows = dot(from_recv, shufr[b].reshape(128, eighth)).astype(BF)
        gath[b, x] = jnp.concatenate([rows[k * 16:(k + 1) * 16, :] for k in range(8)], axis=1)
        mine = gath.at[b, x]
        remote(mine, mine, gsend.at[b, 0], grecv.at[b, 0], right).start()
        remote(mine, mine, gsend.at[b, 1], grecv.at[b, 1], left).start()

    def gather_relay(b):
        from_left, from_right = gath.at[b, xl], gath.at[b, xr]
        remote(from_left, from_left, gsend.at[b, 0], grecv.at[b, 0], right).wait_recv()
        piece = gath.at[b, xl, :, lo]
        remote(piece, piece, gsend.at[b, 2], grecv.at[b, 2], right).start()
        remote(from_right, from_right, gsend.at[b, 1], grecv.at[b, 1], left).wait_recv()
        piece = gath.at[b, xr, :, hi]
        remote(piece, piece, gsend.at[b, 3], grecv.at[b, 3], left).start()

    def temporal(lead, last):
        n = (last - lead) * 64
        for b in range(lead, last):
            far = gath.at[b, xo]
            remote(far.at[:, lo], far.at[:, lo], gsend.at[b, 2], grecv.at[b, 2], right).wait_recv()
            remote(far.at[:, hi], far.at[:, hi], gsend.at[b, 3], grecv.at[b, 3], left).wait_recv()
        rows = gath[lead:last].reshape(n, d).astype(F32)
        center = rows - jnp.sum(rows, axis=1, keepdims=True) * (1.0 / d)
        spread = jnp.sum(center * center, axis=1, keepdims=True) * (1.0 / d)
        scale = lax.rsqrt(spread + 1e-06)
        normed = (center * scale * (1.0 + tmod[1:2, :]) + tmod[0:1, :]).astype(BF)
        if lead == 0:
            weight_end(1)
        joined = dot(normed, wt[...].reshape(d, 1536)).astype(BF)
        same = (iota((n, n), 0) >> 3) == (iota((n, n), 1) >> 3)
        attended = []
        for j in range(4):
            mine = joined[:, j * 384:(j + 1) * 384]
            scores = jnp.where(same, dot_nt(mine[:, 0:128], mine[:, 128:256]), -1e30)
            top = jnp.max(scores, axis=1, keepdims=True)
            probs = jnp.exp2((scores - top) * score_scale)
            probs = (probs / jnp.sum(probs, axis=1, keepdims=True)).astype(BF)
            attended.append(dot(probs, mine[:, 256:384]).astype(BF))
        if lead == 0:
            weight_end(2)
        lhs = jnp.concatenate(attended, axis=1)
        part2[lead:last] = dot(lhs, wto[...].reshape(512, d)).astype(BF).reshape(last - lead, 4, 16, d)
        for b in range(lead, last):
            ring_first(b, part2, relay2, got2, rsend2, rrecv2)

    def back_second(b):
        ring_second(b, part2, relay2, got2, rsend2, rrecv2)

    def finish(b):
        total = ring_last(b, part2, got2, rsend2, rrecv2)
        res[b] = (gath[b, x].astype(F32) + tmod[2:3, :] * total).astype(BF)
        rows = pl.ds(pl.multiple_of(b * 16, 16), 16)
        pltpu.make_async_copy(res.at[b], out.at[rows, :], out_sem.at[b]).start()

    def sum_second(b):
        ring_second(b, part, relay, got, rsend, rrecv)

    blocks = {
        "attend": attend, "sum_begin": sum_begin, "sum_second": sum_second, "swap_send": swap_send,
        "gather_send": gather_send, "gather_relay": gather_relay, "back_second": back_second, "finish": finish,
    }
    moves = {"temporal": temporal, "quarter": weight_quarter, "relay": weight_relay, "rest": weight_rest}

    def tick(t, _):
        for name, *what in TABLE:
            if name in blocks:
                hit, b = t < 0, 0
                for when, block in what:
                    hit = hit | (t == when)
                    b = b + jnp.where(t == when, block, 0)

                @pl.when(hit)
                def _(name=name, b=b):
                    blocks[name](b)
            else:
                @pl.when(t == what[0])
                def _(name=name, what=what):
                    moves[name](*what[1:])

        return 0

    lax.fori_loop(0, COUNT, tick, 0)

    for b in range(nb):
        pltpu.make_async_copy(res.at[b], out.at[pl.ds(b * 16, 16), :], out_sem.at[b]).wait()

    def sent(b, _):
        for r in (1, 2, 3):
            remote(cat.at[b, r], cat.at[b, r], asend.at[b, r], arecv.at[b, r], quad[r]).wait_send()
        ring_sent(b, relay, rsend, rrecv)
        ring_sent(b, relay2, rsend2, rrecv2)
        for j in range(1, 8):
            piece = shuf.at[b, 0]
            remote(piece, piece, ssend.at[b, j], srecv.at[b, j], right).wait_send()
        for k in range(4):
            piece = gath.at[b, x] if k < 2 else gath.at[b, x, :, lo]
            remote(piece, piece, gsend.at[b, k], grecv.at[b, k], right).wait_send()
        return 0

    lax.fori_loop(0, nb, sent, 0)
    for w in range(3):
        weight_sent(w)


def shards(
    tokens, spatial_modulation, spatial_weights_in, spatial_weights_out,
    temporal_modulation, temporal_weights_in, temporal_weights_out,
):
    d = tokens.shape[-1]
    nb = BLOCKS
    hb = d // 2
    dma = pltpu.SemaphoreType.DMA
    any_space = pl.BlockSpec(memory_space=pl.ANY)
    vmem = pl.BlockSpec(memory_space=pltpu.VMEM)
    out_weights = pltpu.VMEM((4, 4, 2, 16, d), BF)
    ring = [
        pltpu.VMEM((nb, 4, 16, d), BF),
        pltpu.VMEM((nb, 2, 16, hb), BF),
        pltpu.VMEM((nb, 2, 2, 16, hb), BF),
    ]
    result = pl.pallas_call(
        kernel,
        out_shape=jax.ShapeDtypeStruct((80, d), BF),
        in_specs=[any_space, vmem, any_space, any_space, vmem, any_space, any_space],
        out_specs=any_space,
        scratch_shapes=[
            pltpu.VMEM((4, 336, d), BF),
            pltpu.VMEM((16, d), BF),
            pltpu.VMEM((d, 384), BF),
            pltpu.VMEM((d, 512), BF),
            pltpu.VMEM((1280, 128), BF),
            pltpu.VMEM((1280, 128), BF),
            pltpu.VMEM((1280, 256), BF),
            pltpu.VMEM((nb, 4, 64, 128), BF),
            pltpu.VMEM((nb, 4, 64, 128), BF),
            pltpu.VMEM((80, d), BF),
            out_weights,
            pltpu.VMEM((4, 4, d // 16, 1536), BF),
            out_weights,
            *ring,
            pltpu.VMEM((nb, 8, 16, d // 8), BF),
            pltpu.VMEM((nb, 8, 16, d // 8), BF),
            pltpu.VMEM((nb, 4, 16, d), BF),
            *ring,
            pltpu.VMEM((nb, 16, d), BF),
            dma((3,)), dma((4,)), dma((nb,)), dma(()),
            dma((3, 9, 4)), dma((3, 9, 4)),
            dma((nb, 4)), dma((nb, 4)),
            dma((nb, 6)), dma((nb, 6)),
            dma((nb, 8)), dma((nb, 8)),
            dma((nb, 4)), dma((nb, 4)),
            dma((nb, 6)), dma((nb, 6)),
        ],
        compiler_params=pltpu.CompilerParams(
            collective_id=0, has_side_effects=True, vmem_limit_bytes=60 * 1024 * 1024
        ),
        cost_estimate=pl.CostEstimate(
            flops=9_000_000_000, bytes_accessed=16_000_000, transcendentals=2_000_000
        ),
    )(
        tokens.reshape(4, 320, d),
        spatial_modulation,
        jnp.transpose(spatial_weights_in, (1, 0, 2)).reshape(d, 384),
        spatial_weights_out.reshape(4, 2, 16, d),
        temporal_modulation,
        jnp.transpose(temporal_weights_in, (1, 0, 2)).reshape(4, 4, d // 16, 384),
        temporal_weights_out.reshape(4, 2, 16, d),
    )
    return jnp.transpose(result.reshape(10, 8, d), (1, 0, 2))


def solution(mesh):
    placed = (
        P("seq", None, None),
        P(),
        P(None, "head", None),
        P("head", None, None),
        P(),
        P(None, "head", None),
        P("head", None, None),
    )
    return jax.shard_map(
        shards,
        mesh=mesh,
        in_specs=placed,
        out_specs=P(None, ("seq", "head"), None),
        check_vma=False,
    )
```

```python
import functools

import jax
import jax.numpy as jnp
from jax import lax
from jax.experimental import pallas as pl
from jax.experimental.pallas import tpu as pltpu
from jax.sharding import PartitionSpec as P

BF = jnp.bfloat16
F32 = jnp.float32
MESH = pl.DeviceIdType.MESH
BLOCKS = 5
LOG2E = 1.4426950408889634
TABLE = (
    ("attend", (0, 0), (1, 1), (2, 2), (5, 3), (6, 4)),
    ("rest", 1, 0),
    ("sum_begin", (3, 0), (4, 1), (5, 2), (7, 3), (8, 4)),
    ("sum_second", (5, 0), (6, 1), (7, 2), (8, 3), (10, 4)),
    ("swap_send", (7, 0), (8, 1), (9, 2), (10, 3), (12, 4)),
    ("gather_send", (9, 0), (10, 1), (11, 2), (12, 3), (14, 4)),
    ("gather_relay", (11, 0), (12, 1), (13, 2), (14, 3), (15, 4)),
    ("rest", 13, 1),
    ("rest", 13, 2),
    ("temporal", 14, 0, 2),
    ("temporal", 15, 2, 4),
    ("temporal", 17, 4, 5),
    ("back_second", (15, 0), (16, 1), (17, 2), (18, 3), (19, 4)),
    ("drain", 19),
    ("finish", (17, 0), (18, 1), (19, 2), (20, 3), (21, 4)),
    ("quarter", 0, 1, 0),
    ("quarter", 2, 1, 1),
    ("quarter", 4, 1, 2),
    ("quarter", 5, 1, 3),
    ("quarter", 6, 2, 0),
    ("quarter", 7, 2, 1),
    ("relay", 9, 1, 0),
    ("relay", 10, 1, 1),
    ("relay", 12, 2, 0),
)
COUNT = 22


def dot(a, b):
    return jnp.dot(a, b, preferred_element_type=F32)


def dot_nt(a, b):
    return lax.dot_general(a, b, (((1,), (1,)), ((), ())), preferred_element_type=F32)


def iota(shape, axis):
    return lax.broadcasted_iota(jnp.int32, shape, axis)


def one_hot(hit):
    return jnp.where(hit, 1.0, 0.0).astype(BF)


def remote(src, dst, send, recv, device):
    return pltpu.make_async_remote_copy(
        src_ref=src, dst_ref=dst, send_sem=send, recv_sem=recv,
        device_id=device, device_id_type=MESH,
    )


def kernel(
    tok_in, smod, win_in, wo_in, tmod, wt_in, wto_in,
    out,
    tok, shift, wi, wx, qb, kb, vx, att, cat, own_rows, wo, wt, wto,
    part, relay, got, shuf, shufr, gath, tnorm, part2, relay2, got2, res,
    local_sem, tok_sem, out_sem, win_sem, wsend, wrecv, asend, arecv,
    rsend, rrecv, ssend, srecv, gsend, grecv, rsend2, rrecv2,
):
    d = tok.shape[-1]
    nb = BLOCKS
    hb = d // 2
    eighth = d // 8
    s = lax.axis_index("seq")
    h = lax.axis_index("head")
    yl, z = s // 4, s % 4
    x, q = h // 4, h % 4
    yh, core = q // 2, q % 2
    right = (s, ((x + 1) % 4) * 4 + q)
    left = (s, ((x + 3) % 4) * 4 + q)
    quarters = [((yh + r // 2) % 2) * 2 + (core + r) % 2 for r in range(4)]
    quad = [(s, x * 4 + k) for k in quarters]
    mate = quad[1]
    cross = ((1 - yl) * 4 + z, x * 4 + (1 - yh) * 2 + core)
    beside = ((1 - yl) * 4 + z, h)
    up = (yl * 4 + (z + 1) % 4, h)
    down = (yl * 4 + (z + 3) % 4, h)
    xr, xl, xo = (x + 1) % 4, (x + 3) % 4, (x + 2) % 4
    zu, zd, zo = (z + 1) % 4, (z + 3) % 4, (z + 2) % 4

    barrier = pltpu.get_barrier_semaphore()
    partners = [right, left] + quad[1:] + [cross] + [((s + j) % 8, h) for j in range(1, 8)]
    for device in partners:
        pl.semaphore_signal(barrier, inc=1, device_id=device, device_id_type=MESH)

    load_w = pltpu.make_async_copy(win_in, wi, win_sem)
    load_w.start()
    for i in range(4):
        pltpu.make_async_copy(tok_in.at[i], tok.at[i, pl.ds(0, 320)], tok_sem.at[i]).start()
    weights = ((wo_in, wo), (wt_in, wt), (wto_in, wto))
    own_loads = [
        pltpu.make_async_copy(wo_in, wo.at[0], local_sem.at[0]),
        pltpu.make_async_copy(wt_in, wt.at[:, :, :, pl.ds(0, 384)], local_sem.at[1]),
        pltpu.make_async_copy(wto_in, wto.at[0], local_sem.at[2]),
    ]
    for load in own_loads:
        load.start()

    counts = (2, 4, 2)

    def at(w, slot, *where):
        buf = weights[w][1]
        if w == 1:
            where = where + (slice(None),) * (3 - len(where))
            return buf.at[where + (pl.ds(slot * 384, 384),)]
        return buf.at[(slot,) + where]

    def copy_of(w, kind, k, piece, to, device):
        return remote(piece, to, wsend.at[w, kind, k], wrecv.at[w, kind, k], device)

    def first_quarter(step):
        return (z + 2 * yl + step) % 4

    def weight_near(w):
        copy_of(w, 0, 0, weights[w][0], at(w, 1), mate).start()

    def weight_cross(w):
        for k in range(counts[w]):
            quarter = z if w else first_quarter(2)
            copy_of(w, 1, k, weights[w][0].at[quarter, k], at(w, 2, quarter, k), cross).start()

    def weight_quarter(w, k):
        quarter = z if w else first_quarter(0)
        piece = at(w, 2, quarter, k)
        copy_of(w, 1, k, piece, piece, cross).wait_recv()
        copy_of(w, 3, k, piece, piece, up).start()
        copy_of(w, 4, k, piece, piece, down).start()
        if w == 0:
            copy_of(w, 6, k, piece, piece, beside).start()
        copy_of(w, 5, k, piece, at(w, 3, quarter, k), mate).start()

    def weight_relay(w, k):
        m = counts[w] // 2
        below, above = at(w, 2, zd, k), at(w, 2, zu, m + k)
        copy_of(w, 3, k, below, below, up).wait_recv()
        copy_of(w, 6, k, below, below, up).start()
        copy_of(w, 4, m + k, above, above, down).wait_recv()
        copy_of(w, 7, k, above, above, down).start()

    def weight_rest(w):
        if w == 0:
            for j, kind, step in ((0, 3, 3), (1, 4, 1), (2, 6, 2)):
                quarter = first_quarter(step)
                for k in range(counts[w]):
                    piece = at(w, 2, quarter, k)
                    copy_of(w, kind, k, piece, piece, up).wait_recv()
                copy_of(w, 8, j, at(w, 2, quarter), at(w, 3, quarter), mate).start()
            return
        m = counts[w] // 2
        for k in range(m, 2 * m):
            piece = at(w, 2, zd, k)
            copy_of(w, 3, k, piece, piece, up).wait_recv()
        copy_of(w, 8, 0, at(w, 2, zd), at(w, 3, zd), mate).start()
        for k in range(m):
            piece = at(w, 2, zu, k)
            copy_of(w, 4, k, piece, piece, down).wait_recv()
        copy_of(w, 8, 1, at(w, 2, zu), at(w, 3, zu), mate).start()
        for k in range(m):
            piece = at(w, 2, zo, k)
            copy_of(w, 6, k, piece, piece, up).wait_recv()
            piece = at(w, 2, zo, m + k)
            copy_of(w, 7, k, piece, piece, down).wait_recv()
        copy_of(w, 8, 2, at(w, 2, zo), at(w, 3, zo), mate).start()

    def weight_end(w):
        own_loads[w].wait()
        copy_of(w, 0, 0, weights[w][0], at(w, 1), mate).wait_recv()
        near, rest = (z, (zd, zu, zo)) if w else (first_quarter(0), [first_quarter(k) for k in (3, 1, 2)])
        for k in range(counts[w]):
            copy_of(w, 5, k, at(w, 3, near, k), at(w, 3, near, k), mate).wait_recv()
        for k, quarter in enumerate(rest):
            copy_of(w, 8, k, at(w, 3, quarter), at(w, 3, quarter), mate).wait_recv()

    def weight_sent(w):
        piece, whole = at(w, 2, z, 0), at(w, 2, z)
        copy_of(w, 0, 0, weights[w][0], at(w, 1), mate).wait_send()
        for kind in (1, 3, 4, 5):
            for k in range(counts[w]):
                copy_of(w, kind, k, piece, piece, up).wait_send()
        for k in range(2 if w == 0 else counts[w] // 2):
            copy_of(w, 6, k, piece, piece, up).wait_send()
            if w:
                copy_of(w, 7, k, piece, piece, down).wait_send()
        for k in range(3):
            copy_of(w, 8, k, whole, whole, mate).wait_send()

    pl.semaphore_wait(barrier, len(partners))
    for w in range(3):
        weight_cross(w)
    for w in range(3):
        weight_near(w)

    load_w.wait()
    m0 = smod[0:1, :]
    m0_high = m0.astype(BF).astype(F32)
    row = iota((16, d), 0)
    shift_rows = jnp.where(row == 0, m0_high, jnp.where(row == 1, m0 - m0_high, 0.0)).astype(BF)
    shift[...] = shift_rows

    def fold(i, total):
        rows = pl.ds(pl.multiple_of(i * 128, 128), 128)
        gain = jnp.broadcast_to(1.0 + smod[1:2, rows], (128, 128)).T
        for j in range(3):
            cols = slice(j * 128, (j + 1) * 128)
            wx[rows, cols] = (wi[rows, cols].astype(F32) * gain).astype(BF)
        wx[rows, 384:512] = jnp.ones((128, 128), BF)
        return total + dot(shift[:, rows], wi[rows, :])

    bias = lax.fori_loop(0, d // 128, fold, jnp.zeros((16, 384), F32), unroll=4)
    bias = jnp.sum(bias, axis=0, keepdims=True)
    tok[:, 320:336] = jnp.ones((4, 16, d), BF)

    def project(i, _):
        pltpu.make_async_copy(tok_in.at[i], tok.at[i, pl.ds(0, 320)], tok_sem.at[i]).wait()

        @pl.when(i == 2)
        def _():
            weight_quarter(0, 0)

        @pl.when(i == 3)
        def _():
            weight_quarter(0, 1)

        every = dot(tok[i], wx[...])
        raw, colsum = every[0:320], every[320:321, 0:384]
        t = tok[i, 0:320]
        base = t[:, 0:1].astype(F32)
        squares = jnp.zeros((320, 128), F32)
        for j in range(d // 128):
            e = t[:, j * 128:(j + 1) * 128].astype(F32) - base
            squares = squares + e * e
        mean = raw[:, 384:385] * (1.0 / d)
        spread = jnp.sum(squares, axis=1, keepdims=True) * (1.0 / d) - (mean - base) * (mean - base)
        scale = lax.rsqrt(spread + 1e-06)
        full = ((raw[:, 0:384] - mean * colsum) * scale + bias).astype(BF)
        rows = pl.ds(pl.multiple_of(i * 320, 320), 320)
        qb[rows, :] = full[:, 0:128]
        kb[rows, :] = full[:, 128:256]
        vx[rows, 0:128] = full[:, 256:384]
        vx[rows, 128:256] = jnp.ones((320, 128), BF)
        return 0

    lax.fori_loop(0, 4, project, 0)

    score_scale = 128 ** (-0.5) * LOG2E

    r256 = iota((256, 1), 0)
    spot = ((r256 >> 1) & 7) * 160 + ((r256 >> 4) & 3) * 40 + (r256 >> 6) * 10 + (r256 & 1)
    cells = iota((1, 1280), 1)

    def attend(b):
        queries = dot(one_hot(spot + 2 * b == cells), qb[...]).astype(BF)
        scores = dot_nt(queries, kb[...])
        top = jnp.max(scores, axis=1, keepdims=True)
        probs = jnp.exp2((scores - top) * score_scale).astype(BF)
        both = dot(probs, vx[...])
        att[b] = (both[:, 0:128] / both[:, 128:256]).astype(BF).reshape(4, 64, 128)
        for r in (2, 3, 1):
            remote(att.at[b, quarters[r]], cat.at[b, r], asend.at[b, r], arecv.at[b, r], quad[r]).start()


    first = h * 10
    start = jnp.minimum((first // 16) * 16, 128)
    skip = first - start
    r80 = iota((80, 1), 0)
    target = ((r80 >> 1) & 7) * 32 + (r80 >> 4) * 2 + (r80 & 1) + skip
    windows = jnp.concatenate(
        [tok[k // 2, pl.ds(pl.multiple_of((k % 2) * 160 + start, 16), 32), :] for k in range(8)], axis=0
    )
    own_rows[...] = dot(one_hot(target == iota((1, 256), 1)), windows).astype(BF)

    r128 = iota((128, 1), 0)
    c128 = iota((1, 128), 1)
    to_send = one_hot((r128 & 7) * 16 + (r128 >> 4) * 2 + ((r128 >> 3) & 1) == c128)
    from_recv = one_hot((r128 & 7) * 16 + ((r128 >> 3) & 1) * 8 + (r128 >> 4) == c128)
    lo, hi = pl.ds(0, hb), pl.ds(hb, hb)

    def ring_first(b, half, buf, rel, rec, ss, rs):
        if half == 0:
            remote(buf.at[b, xo, :, lo], rel.at[b, 0], ss.at[b, 0], rs.at[b, 0], right).start()
            remote(buf.at[b, xl, :, lo], rec.at[b, 1, 0], ss.at[b, 3], rs.at[b, 3], left).start()
        else:
            remote(buf.at[b, xo, :, hi], rel.at[b, 1], ss.at[b, 1], rs.at[b, 1], left).start()
            remote(buf.at[b, xr, :, hi], rec.at[b, 0, 1], ss.at[b, 2], rs.at[b, 2], right).start()

    def ring_second(b, buf, rel, rec, ss, rs):
        remote(rel.at[b, 0], rel.at[b, 0], ss.at[b, 0], rs.at[b, 0], right).wait_recv()
        rel[b, 0] = (rel[b, 0].astype(F32) + buf[b, xr, :, lo].astype(F32)).astype(BF)
        remote(rel.at[b, 0], rec.at[b, 0, 0], ss.at[b, 4], rs.at[b, 4], right).start()
        remote(rel.at[b, 1], rel.at[b, 1], ss.at[b, 1], rs.at[b, 1], left).wait_recv()
        rel[b, 1] = (rel[b, 1].astype(F32) + buf[b, xl, :, hi].astype(F32)).astype(BF)
        remote(rel.at[b, 1], rec.at[b, 1, 1], ss.at[b, 5], rs.at[b, 5], left).start()

    def ring_last(b, buf, rec, ss, rs):
        for k, side, half in ((2, 0, 1), (3, 1, 0), (4, 0, 0), (5, 1, 1)):
            piece = rec.at[b, side, half]
            remote(piece, piece, ss.at[b, k], rs.at[b, k], right).wait_recv()
        own = buf[b, x].astype(F32)
        halves = [
            own[:, k * hb:(k + 1) * hb] + rec[b, 0, k].astype(F32) + rec[b, 1, k].astype(F32)
            for k in range(2)
        ]
        return jnp.concatenate(halves, axis=1)

    def ring_sent(b, rel, ss, rs):
        for k in range(6):
            remote(rel.at[b, 0], rel.at[b, 0], ss.at[b, k], rs.at[b, k], right).wait_send()

    def sum_begin(b):
        @pl.when(b == 0)
        def _():
            weight_end(0)

        for r in (1, 2, 3):
            remote(cat.at[b, r], cat.at[b, r], asend.at[b, r], arecv.at[b, r], quad[r]).wait_recv()
        lhs = jnp.concatenate([att[b, q], cat[b, 1], cat[b, 2], cat[b, 3]], axis=1)
        for half, cols in ((0, lo), (1, hi)):
            part[b, :, :, cols] = dot(lhs, wo[:, :, :, :, cols].reshape(512, hb)).astype(BF).reshape(4, 16, hb)
            ring_first(b, half, part, relay, got, rsend, rrecv)

    def swap_send(b):
        total = ring_last(b, part, got, rsend, rrecv)
        rows = own_rows[pl.ds(pl.multiple_of(b * 16, 16), 16), :]
        middle = (rows.astype(F32) + smod[2:3, :] * total).astype(BF)
        stacked = jnp.concatenate([middle[:, k * eighth:(k + 1) * eighth] for k in range(8)], axis=0)
        shuf[b] = dot(to_send, stacked).astype(BF).reshape(8, 16, eighth)
        for j in (2, 6, 3, 5, 1, 7, 4):
            to = (s + j) % 8
            remote(shuf.at[b, to], shufr.at[b, s], ssend.at[b, j], srecv.at[b, j], (to, h)).start()
        shufr[b, s] = shuf[b, s]

    def gather_send(b):
        for j in range(1, 8):
            piece = shufr.at[b, (s + 8 - j) % 8]
            remote(piece, piece, ssend.at[b, j], srecv.at[b, j], right).wait_recv()
        rows = dot(from_recv, shufr[b].reshape(128, eighth)).astype(BF)
        gath[b, x] = jnp.concatenate([rows[k * 16:(k + 1) * 16, :] for k in range(8)], axis=1)
        mine = gath.at[b, x]
        remote(mine, mine, gsend.at[b, 0], grecv.at[b, 0], right).start()
        remote(mine, mine, gsend.at[b, 1], grecv.at[b, 1], left).start()

    def gather_relay(b):
        from_left, from_right = gath.at[b, xl], gath.at[b, xr]
        remote(from_left, from_left, gsend.at[b, 0], grecv.at[b, 0], right).wait_recv()
        piece = gath.at[b, xl, :, lo]
        remote(piece, piece, gsend.at[b, 2], grecv.at[b, 2], right).start()
        remote(from_right, from_right, gsend.at[b, 1], grecv.at[b, 1], left).wait_recv()
        piece = gath.at[b, xr, :, hi]
        remote(piece, piece, gsend.at[b, 3], grecv.at[b, 3], left).start()

    def temporal(lead, last):
        n = (last - lead) * 64
        for b in range(lead, last):
            far = gath.at[b, xo]
            remote(far.at[:, lo], far.at[:, lo], gsend.at[b, 2], grecv.at[b, 2], right).wait_recv()
            remote(far.at[:, hi], far.at[:, hi], gsend.at[b, 3], grecv.at[b, 3], left).wait_recv()
        rows = gath[lead:last].reshape(n, d)
        base = rows[:, 0:1].astype(F32)
        total, squares = jnp.zeros((n, 128), F32), jnp.zeros((n, 128), F32)
        for k in range(d // 128):
            e = rows[:, k * 128:(k + 1) * 128].astype(F32) - base
            total, squares = total + e, squares + e * e
        off = jnp.sum(total, axis=1, keepdims=True) * (1.0 / d)
        spread = jnp.sum(squares, axis=1, keepdims=True) * (1.0 / d) - off * off
        scale = lax.rsqrt(spread + 1e-06)
        mean = base + off
        for k in range(d // 128):
            cols = slice(k * 128, (k + 1) * 128)
            center = (rows[:, cols].astype(F32) - mean) * scale
            tnorm[0:n, cols] = (center * (1.0 + tmod[1:2, cols]) + tmod[0:1, cols]).astype(BF)
        if lead == 0:
            weight_end(1)
        joined = dot(tnorm[0:n], wt[...].reshape(d, 1536)).astype(BF)
        same = (iota((n, n), 0) >> 3) == (iota((n, n), 1) >> 3)
        attended = []
        for j in range(4):
            mine = joined[:, j * 384:(j + 1) * 384]
            scores = jnp.where(same, dot_nt(mine[:, 0:128], mine[:, 128:256]), -1e30)
            top = jnp.max(scores, axis=1, keepdims=True)
            probs = jnp.exp2((scores - top) * score_scale)
            probs = (probs / jnp.sum(probs, axis=1, keepdims=True)).astype(BF)
            attended.append(dot(probs, mine[:, 256:384]).astype(BF))
        if lead == 0:
            weight_end(2)
        lhs = jnp.concatenate(attended, axis=1)
        for half, cols in ((0, lo), (1, hi)):
            some = dot(lhs, wto[:, :, :, :, cols].reshape(512, hb)).astype(BF)
            part2[lead:last, :, :, cols] = some.reshape(last - lead, 4, 16, hb)
            for b in range(lead, last):
                ring_first(b, half, part2, relay2, got2, rsend2, rrecv2)

    def back_second(b):
        ring_second(b, part2, relay2, got2, rsend2, rrecv2)

    def finish(b):
        total = ring_last(b, part2, got2, rsend2, rrecv2)
        res[b] = (gath[b, x].astype(F32) + tmod[2:3, :] * total).astype(BF)
        rows = pl.ds(pl.multiple_of(b * 16, 16), 16)
        pltpu.make_async_copy(res.at[b], out.at[rows, :], out_sem.at[b]).start()

    def sum_second(b):
        ring_second(b, part, relay, got, rsend, rrecv)

    def sent(b, _):
        for r in (1, 2, 3):
            remote(cat.at[b, r], cat.at[b, r], asend.at[b, r], arecv.at[b, r], quad[r]).wait_send()
        ring_sent(b, relay, rsend, rrecv)
        for j in range(1, 8):
            piece = shuf.at[b, 0]
            remote(piece, piece, ssend.at[b, j], srecv.at[b, j], right).wait_send()
        for k in range(4):
            piece = gath.at[b, x] if k < 2 else gath.at[b, x, :, lo]
            remote(piece, piece, gsend.at[b, k], grecv.at[b, k], right).wait_send()
        return 0

    def drain():
        lax.fori_loop(0, nb, sent, 0)
        for w in range(3):
            weight_sent(w)

    blocks = {
        "attend": attend, "sum_begin": sum_begin, "sum_second": sum_second, "swap_send": swap_send,
        "gather_send": gather_send, "gather_relay": gather_relay, "back_second": back_second, "finish": finish,
    }
    moves = {"temporal": temporal, "quarter": weight_quarter, "relay": weight_relay, "rest": weight_rest,
        "drain": drain}

    def tick(t, _):
        for name, *what in TABLE:
            if name in blocks:
                hit, b = t < 0, 0
                for when, block in what:
                    hit = hit | (t == when)
                    b = b + jnp.where(t == when, block, 0)

                @pl.when(hit)
                def _(name=name, b=b):
                    blocks[name](b)
            else:
                @pl.when(t == what[0])
                def _(name=name, what=what):
                    moves[name](*what[1:])

        return 0

    lax.fori_loop(0, COUNT, tick, 0)

    for b in range(nb):
        pltpu.make_async_copy(res.at[b], out.at[pl.ds(b * 16, 16), :], out_sem.at[b]).wait()

    def back_sent(b, _):
        ring_sent(b, relay2, rsend2, rrecv2)
        return 0

    lax.fori_loop(0, nb, back_sent, 0)


def shards(
    tokens, spatial_modulation, spatial_weights_in, spatial_weights_out,
    temporal_modulation, temporal_weights_in, temporal_weights_out,
):
    d = tokens.shape[-1]
    nb = BLOCKS
    hb = d // 2
    dma = pltpu.SemaphoreType.DMA
    any_space = pl.BlockSpec(memory_space=pl.ANY)
    vmem = pl.BlockSpec(memory_space=pltpu.VMEM)
    out_weights = pltpu.VMEM((4, 4, 2, 16, d), BF)
    ring = [
        pltpu.VMEM((nb, 4, 16, d), BF),
        pltpu.VMEM((nb, 2, 16, hb), BF),
        pltpu.VMEM((nb, 2, 2, 16, hb), BF),
    ]
    result = pl.pallas_call(
        kernel,
        out_shape=jax.ShapeDtypeStruct((80, d), BF),
        in_specs=[any_space, vmem, any_space, any_space, vmem, any_space, any_space],
        out_specs=any_space,
        scratch_shapes=[
            pltpu.VMEM((4, 336, d), BF),
            pltpu.VMEM((16, d), BF),
            pltpu.VMEM((d, 384), BF),
            pltpu.VMEM((d, 512), BF),
            pltpu.VMEM((1280, 128), BF),
            pltpu.VMEM((1280, 128), BF),
            pltpu.VMEM((1280, 256), BF),
            pltpu.VMEM((nb, 4, 64, 128), BF),
            pltpu.VMEM((nb, 4, 64, 128), BF),
            pltpu.VMEM((80, d), BF),
            out_weights,
            pltpu.VMEM((4, 4, d // 16, 1536), BF),
            out_weights,
            *ring,
            pltpu.VMEM((nb, 8, 16, d // 8), BF),
            pltpu.VMEM((nb, 8, 16, d // 8), BF),
            pltpu.VMEM((nb, 4, 16, d), BF),
            pltpu.VMEM((nb * 64, d), BF),
            *ring,
            pltpu.VMEM((nb, 16, d), BF),
            dma((3,)), dma((4,)), dma((nb,)), dma(()),
            dma((3, 9, 4)), dma((3, 9, 4)),
            dma((nb, 4)), dma((nb, 4)),
            dma((nb, 6)), dma((nb, 6)),
            dma((nb, 8)), dma((nb, 8)),
            dma((nb, 4)), dma((nb, 4)),
            dma((nb, 6)), dma((nb, 6)),
        ],
        compiler_params=pltpu.CompilerParams(
            collective_id=0, has_side_effects=True, vmem_limit_bytes=60 * 1024 * 1024
        ),
        cost_estimate=pl.CostEstimate(
            flops=9_000_000_000, bytes_accessed=16_000_000, transcendentals=2_000_000
        ),
    )(
        tokens.reshape(4, 320, d),
        spatial_modulation,
        jnp.transpose(spatial_weights_in, (1, 0, 2)).reshape(d, 384),
        spatial_weights_out.reshape(4, 2, 16, d),
        temporal_modulation,
        jnp.transpose(temporal_weights_in, (1, 0, 2)).reshape(4, 4, d // 16, 384),
        temporal_weights_out.reshape(4, 2, 16, d),
    )
    return jnp.transpose(result.reshape(10, 8, d), (1, 0, 2))


def solution(mesh):
    placed = (
        P("seq", None, None),
        P(),
        P(None, "head", None),
        P("head", None, None),
        P(),
        P(None, "head", None),
        P("head", None, None),
    )
    return jax.shard_map(
        shards,
        mesh=mesh,
        in_specs=placed,
        out_specs=P(None, ("seq", "head"), None),
        check_vma=False,
    )
```

```python
import functools

import jax
import jax.numpy as jnp
from jax import lax
from jax.experimental import pallas as pl
from jax.experimental.pallas import tpu as pltpu
from jax.sharding import PartitionSpec as P

BF = jnp.bfloat16
F32 = jnp.float32
MESH = pl.DeviceIdType.MESH
BLOCKS = 5
LOG2E = 1.4426950408889634
TABLE = (
    ("attend", (0, 0), (1, 1), (2, 2), (5, 3), (6, 4)),
    ("rest", 1, 0),
    ("sum_begin", (3, 0), (4, 1), (5, 2), (7, 3), (8, 4)),
    ("sum_second", (5, 0), (6, 1), (7, 2), (8, 3), (10, 4)),
    ("swap_send", (7, 0), (8, 1), (9, 2), (10, 3), (12, 4)),
    ("gather_send", (9, 0), (10, 1), (11, 2), (12, 3), (14, 4)),
    ("gather_relay", (11, 0), (12, 1), (13, 2), (14, 3), (15, 4)),
    ("rest", 13, 1),
    ("rest", 13, 2),
    ("temporal", 14, 0, 2),
    ("temporal", 15, 2, 4),
    ("temporal", 17, 4, 5),
    ("back_second", (15, 0), (16, 1), (17, 2), (18, 3), (19, 4)),
    ("drain", 19),
    ("finish", (17, 0), (18, 1), (19, 2), (20, 3), (21, 4)),
    ("quarter", 0, 1, 0),
    ("quarter", 2, 1, 1),
    ("quarter", 4, 1, 2),
    ("quarter", 5, 1, 3),
    ("quarter", 6, 2, 0),
    ("quarter", 7, 2, 1),
    ("relay", 9, 1, 0),
    ("relay", 10, 1, 1),
    ("relay", 12, 2, 0),
)
COUNT = 22


def dot(a, b):
    return jnp.dot(a, b, preferred_element_type=F32)


def dot_nt(a, b):
    return lax.dot_general(a, b, (((1,), (1,)), ((), ())), preferred_element_type=F32)


def iota(shape, axis):
    return lax.broadcasted_iota(jnp.int32, shape, axis)


def one_hot(hit):
    return jnp.where(hit, 1.0, 0.0).astype(BF)


def remote(src, dst, send, recv, device):
    return pltpu.make_async_remote_copy(
        src_ref=src, dst_ref=dst, send_sem=send, recv_sem=recv,
        device_id=device, device_id_type=MESH,
    )


def kernel(
    tok_in, smod, win_in, wo_in, tmod, wt_in, wto_in,
    out,
    tok, shift, wi, wx, qb, kb, vx, att, cat, own_rows, wo, wt, wto,
    part, relay, got, shuf, shufr, gath, tnorm, part2, relay2, got2, res,
    local_sem, tok_sem, out_sem, win_sem, wsend, wrecv, asend, arecv,
    rsend, rrecv, ssend, srecv, gsend, grecv, rsend2, rrecv2,
):
    d = tok.shape[-1]
    nb = BLOCKS
    hb = d // 2
    eighth = d // 8
    s = lax.axis_index("seq")
    h = lax.axis_index("head")
    yl, z = s // 4, s % 4
    x, q = h // 4, h % 4
    yh, core = q // 2, q % 2
    right = (s, ((x + 1) % 4) * 4 + q)
    left = (s, ((x + 3) % 4) * 4 + q)
    quarters = [((yh + r // 2) % 2) * 2 + (core + r) % 2 for r in range(4)]
    quad = [(s, x * 4 + k) for k in quarters]
    mate = quad[1]
    cross = ((1 - yl) * 4 + z, x * 4 + (1 - yh) * 2 + core)
    beside = ((1 - yl) * 4 + z, h)
    up = (yl * 4 + (z + 1) % 4, h)
    down = (yl * 4 + (z + 3) % 4, h)
    xr, xl, xo = (x + 1) % 4, (x + 3) % 4, (x + 2) % 4
    zu, zd, zo = (z + 1) % 4, (z + 3) % 4, (z + 2) % 4

    barrier = pltpu.get_barrier_semaphore()
    partners = [right, left] + quad[1:] + [cross] + [((s + j) % 8, h) for j in range(1, 8)]
    for device in partners:
        pl.semaphore_signal(barrier, inc=1, device_id=device, device_id_type=MESH)

    load_w = pltpu.make_async_copy(win_in, wi, win_sem)
    load_w.start()
    for i in range(4):
        pltpu.make_async_copy(tok_in.at[i], tok.at[i, pl.ds(0, 320)], tok_sem.at[i]).start()
    weights = ((wo_in, wo), (wt_in, wt), (wto_in, wto))
    own_loads = [
        pltpu.make_async_copy(wo_in, wo.at[0], local_sem.at[0]),
        pltpu.make_async_copy(wt_in, wt.at[:, :, :, pl.ds(0, 384)], local_sem.at[1]),
        pltpu.make_async_copy(wto_in, wto.at[0], local_sem.at[2]),
    ]
    own_loads[0].start()

    counts = (2, 4, 2)

    def at(w, slot, *where):
        buf = weights[w][1]
        if w == 1:
            where = where + (slice(None),) * (3 - len(where))
            return buf.at[where + (pl.ds(slot * 384, 384),)]
        return buf.at[(slot,) + where]

    def copy_of(w, kind, k, piece, to, device):
        return remote(piece, to, wsend.at[w, kind, k], wrecv.at[w, kind, k], device)

    def first_quarter(step):
        return (z + 2 * yl + step) % 4

    def weight_near(w):
        copy_of(w, 0, 0, weights[w][0], at(w, 1), mate).start()

    def weight_cross(w):
        for k in range(counts[w]):
            quarter = z if w else first_quarter(2)
            copy_of(w, 1, k, weights[w][0].at[quarter, k], at(w, 2, quarter, k), cross).start()

    def weight_quarter(w, k):
        quarter = z if w else first_quarter(0)
        piece = at(w, 2, quarter, k)
        copy_of(w, 1, k, piece, piece, cross).wait_recv()
        copy_of(w, 3, k, piece, piece, up).start()
        copy_of(w, 4, k, piece, piece, down).start()
        if w == 0:
            copy_of(w, 6, k, piece, piece, beside).start()
        copy_of(w, 5, k, piece, at(w, 3, quarter, k), mate).start()

    def weight_relay(w, k):
        m = counts[w] // 2
        below, above = at(w, 2, zd, k), at(w, 2, zu, m + k)
        copy_of(w, 3, k, below, below, up).wait_recv()
        copy_of(w, 6, k, below, below, up).start()
        copy_of(w, 4, m + k, above, above, down).wait_recv()
        copy_of(w, 7, k, above, above, down).start()

    def weight_rest(w):
        if w == 0:
            for j, kind, step in ((0, 3, 3), (1, 4, 1), (2, 6, 2)):
                quarter = first_quarter(step)
                for k in range(counts[w]):
                    piece = at(w, 2, quarter, k)
                    copy_of(w, kind, k, piece, piece, up).wait_recv()
                copy_of(w, 8, j, at(w, 2, quarter), at(w, 3, quarter), mate).start()
            return
        m = counts[w] // 2
        for k in range(m, 2 * m):
            piece = at(w, 2, zd, k)
            copy_of(w, 3, k, piece, piece, up).wait_recv()
        copy_of(w, 8, 0, at(w, 2, zd), at(w, 3, zd), mate).start()
        for k in range(m):
            piece = at(w, 2, zu, k)
            copy_of(w, 4, k, piece, piece, down).wait_recv()
        copy_of(w, 8, 1, at(w, 2, zu), at(w, 3, zu), mate).start()
        for k in range(m):
            piece = at(w, 2, zo, k)
            copy_of(w, 6, k, piece, piece, up).wait_recv()
            piece = at(w, 2, zo, m + k)
            copy_of(w, 7, k, piece, piece, down).wait_recv()
        copy_of(w, 8, 2, at(w, 2, zo), at(w, 3, zo), mate).start()

    def weight_end(w):
        own_loads[w].wait()
        copy_of(w, 0, 0, weights[w][0], at(w, 1), mate).wait_recv()
        near, rest = (z, (zd, zu, zo)) if w else (first_quarter(0), [first_quarter(k) for k in (3, 1, 2)])
        for k in range(counts[w]):
            copy_of(w, 5, k, at(w, 3, near, k), at(w, 3, near, k), mate).wait_recv()
        for k, quarter in enumerate(rest):
            copy_of(w, 8, k, at(w, 3, quarter), at(w, 3, quarter), mate).wait_recv()

    def weight_sent(w):
        piece, whole = at(w, 2, z, 0), at(w, 2, z)
        copy_of(w, 0, 0, weights[w][0], at(w, 1), mate).wait_send()
        for kind in (1, 3, 4, 5):
            for k in range(counts[w]):
                copy_of(w, kind, k, piece, piece, up).wait_send()
        for k in range(2 if w == 0 else counts[w] // 2):
            copy_of(w, 6, k, piece, piece, up).wait_send()
            if w:
                copy_of(w, 7, k, piece, piece, down).wait_send()
        for k in range(3):
            copy_of(w, 8, k, whole, whole, mate).wait_send()

    pl.semaphore_wait(barrier, len(partners))
    for w in range(3):
        weight_cross(w)
    weight_near(0)

    load_w.wait()
    m0 = smod[0:1, :]
    m0_high = m0.astype(BF).astype(F32)
    row = iota((16, d), 0)
    shift_rows = jnp.where(row == 0, m0_high, jnp.where(row == 1, m0 - m0_high, 0.0)).astype(BF)
    shift[...] = shift_rows

    def fold(i, total):
        rows = pl.ds(pl.multiple_of(i * 128, 128), 128)
        gain = jnp.broadcast_to(1.0 + smod[1:2, rows], (128, 128)).T
        for j in range(3):
            cols = slice(j * 128, (j + 1) * 128)
            wx[rows, cols] = (wi[rows, cols].astype(F32) * gain).astype(BF)
        wx[rows, 384:512] = jnp.ones((128, 128), BF)
        return total + dot(shift[:, rows], wi[rows, :])

    bias = lax.fori_loop(0, d // 128, fold, jnp.zeros((16, 384), F32), unroll=4)
    bias = jnp.sum(bias, axis=0, keepdims=True)
    tok[:, 320:336] = jnp.ones((4, 16, d), BF)

    def project(i, _):
        pltpu.make_async_copy(tok_in.at[i], tok.at[i, pl.ds(0, 320)], tok_sem.at[i]).wait()

        @pl.when(i == 2)
        def _():
            weight_quarter(0, 0)

        @pl.when(i == 3)
        def _():
            weight_quarter(0, 1)

        every = dot(tok[i], wx[...])
        raw, colsum = every[0:320], every[320:321, 0:384]
        t = tok[i, 0:320]
        base = t[:, 0:1].astype(F32)
        squares = jnp.zeros((320, 128), F32)
        for j in range(d // 128):
            e = t[:, j * 128:(j + 1) * 128].astype(F32) - base
            squares = squares + e * e
        mean = raw[:, 384:385] * (1.0 / d)
        spread = jnp.sum(squares, axis=1, keepdims=True) * (1.0 / d) - (mean - base) * (mean - base)
        scale = lax.rsqrt(spread + 1e-06)
        full = ((raw[:, 0:384] - mean * colsum) * scale + bias).astype(BF)
        rows = pl.ds(pl.multiple_of(i * 320, 320), 320)
        qb[rows, :] = full[:, 0:128]
        kb[rows, :] = full[:, 128:256]
        vx[rows, 0:128] = full[:, 256:384]
        vx[rows, 128:256] = jnp.ones((320, 128), BF)
        return 0

    lax.fori_loop(0, 4, project, 0)
    for w in (1, 2):
        own_loads[w].start()
        weight_near(w)

    score_scale = 128 ** (-0.5) * LOG2E

    r256 = iota((256, 1), 0)
    spot = ((r256 >> 1) & 7) * 160 + ((r256 >> 4) & 3) * 40 + (r256 >> 6) * 10 + (r256 & 1)
    cells = iota((1, 1280), 1)

    def attend(b):
        queries = dot(one_hot(spot + 2 * b == cells), qb[...]).astype(BF)
        scores = dot_nt(queries, kb[...])
        top = jnp.max(scores, axis=1, keepdims=True)
        probs = jnp.exp2((scores - top) * score_scale).astype(BF)
        both = dot(probs, vx[...])
        att[b] = (both[:, 0:128] / both[:, 128:256]).astype(BF).reshape(4, 64, 128)
        for r in (2, 3, 1):
            remote(att.at[b, quarters[r]], cat.at[b, r], asend.at[b, r], arecv.at[b, r], quad[r]).start()


    first = h * 10
    start = jnp.minimum((first // 16) * 16, 128)
    skip = first - start
    r80 = iota((80, 1), 0)
    target = ((r80 >> 1) & 7) * 32 + (r80 >> 4) * 2 + (r80 & 1) + skip
    windows = jnp.concatenate(
        [tok[k // 2, pl.ds(pl.multiple_of((k % 2) * 160 + start, 16), 32), :] for k in range(8)], axis=0
    )
    own_rows[...] = dot(one_hot(target == iota((1, 256), 1)), windows).astype(BF)

    r128 = iota((128, 1), 0)
    c128 = iota((1, 128), 1)
    to_send = one_hot((r128 & 7) * 16 + (r128 >> 4) * 2 + ((r128 >> 3) & 1) == c128)
    from_recv = one_hot((r128 & 7) * 16 + ((r128 >> 3) & 1) * 8 + (r128 >> 4) == c128)
    lo, hi = pl.ds(0, hb), pl.ds(hb, hb)

    def ring_first(b, half, buf, rel, rec, ss, rs):
        if half == 0:
            remote(buf.at[b, xo, :, lo], rel.at[b, 0], ss.at[b, 0], rs.at[b, 0], right).start()
            remote(buf.at[b, xl, :, lo], rec.at[b, 1, 0], ss.at[b, 3], rs.at[b, 3], left).start()
        else:
            remote(buf.at[b, xo, :, hi], rel.at[b, 1], ss.at[b, 1], rs.at[b, 1], left).start()
            remote(buf.at[b, xr, :, hi], rec.at[b, 0, 1], ss.at[b, 2], rs.at[b, 2], right).start()

    def ring_second(b, buf, rel, rec, ss, rs):
        remote(rel.at[b, 0], rel.at[b, 0], ss.at[b, 0], rs.at[b, 0], right).wait_recv()
        rel[b, 0] = (rel[b, 0].astype(F32) + buf[b, xr, :, lo].astype(F32)).astype(BF)
        remote(rel.at[b, 0], rec.at[b, 0, 0], ss.at[b, 4], rs.at[b, 4], right).start()
        remote(rel.at[b, 1], rel.at[b, 1], ss.at[b, 1], rs.at[b, 1], left).wait_recv()
        rel[b, 1] = (rel[b, 1].astype(F32) + buf[b, xl, :, hi].astype(F32)).astype(BF)
        remote(rel.at[b, 1], rec.at[b, 1, 1], ss.at[b, 5], rs.at[b, 5], left).start()

    def ring_last(b, buf, rec, ss, rs):
        for k, side, half in ((2, 0, 1), (3, 1, 0), (4, 0, 0), (5, 1, 1)):
            piece = rec.at[b, side, half]
            remote(piece, piece, ss.at[b, k], rs.at[b, k], right).wait_recv()
        own = buf[b, x].astype(F32)
        halves = [
            own[:, k * hb:(k + 1) * hb] + rec[b, 0, k].astype(F32) + rec[b, 1, k].astype(F32)
            for k in range(2)
        ]
        return jnp.concatenate(halves, axis=1)

    def ring_sent(b, rel, ss, rs):
        for k in range(6):
            remote(rel.at[b, 0], rel.at[b, 0], ss.at[b, k], rs.at[b, k], right).wait_send()

    def sum_begin(b):
        @pl.when(b == 0)
        def _():
            weight_end(0)

        for r in (1, 2, 3):
            remote(cat.at[b, r], cat.at[b, r], asend.at[b, r], arecv.at[b, r], quad[r]).wait_recv()
        lhs = jnp.concatenate([att[b, q], cat[b, 1], cat[b, 2], cat[b, 3]], axis=1)
        for half, cols in ((0, lo), (1, hi)):
            part[b, :, :, cols] = dot(lhs, wo[:, :, :, :, cols].reshape(512, hb)).astype(BF).reshape(4, 16, hb)
            ring_first(b, half, part, relay, got, rsend, rrecv)

    def swap_send(b):
        total = ring_last(b, part, got, rsend, rrecv)
        rows = own_rows[pl.ds(pl.multiple_of(b * 16, 16), 16), :]
        middle = (rows.astype(F32) + smod[2:3, :] * total).astype(BF)
        stacked = jnp.concatenate([middle[:, k * eighth:(k + 1) * eighth] for k in range(8)], axis=0)
        shuf[b] = dot(to_send, stacked).astype(BF).reshape(8, 16, eighth)
        for j in (2, 6, 3, 5, 1, 7, 4):
            to = (s + j) % 8
            remote(shuf.at[b, to], shufr.at[b, s], ssend.at[b, j], srecv.at[b, j], (to, h)).start()
        shufr[b, s] = shuf[b, s]

    def gather_send(b):
        for j in range(1, 8):
            piece = shufr.at[b, (s + 8 - j) % 8]
            remote(piece, piece, ssend.at[b, j], srecv.at[b, j], right).wait_recv()
        rows = dot(from_recv, shufr[b].reshape(128, eighth)).astype(BF)
        gath[b, x] = jnp.concatenate([rows[k * 16:(k + 1) * 16, :] for k in range(8)], axis=1)
        mine = gath.at[b, x]
        remote(mine, mine, gsend.at[b, 0], grecv.at[b, 0], right).start()
        remote(mine, mine, gsend.at[b, 1], grecv.at[b, 1], left).start()

    def gather_relay(b):
        from_left, from_right = gath.at[b, xl], gath.at[b, xr]
        remote(from_left, from_left, gsend.at[b, 0], grecv.at[b, 0], right).wait_recv()
        piece = gath.at[b, xl, :, lo]
        remote(piece, piece, gsend.at[b, 2], grecv.at[b, 2], right).start()
        remote(from_right, from_right, gsend.at[b, 1], grecv.at[b, 1], left).wait_recv()
        piece = gath.at[b, xr, :, hi]
        remote(piece, piece, gsend.at[b, 3], grecv.at[b, 3], left).start()

    def temporal(lead, last):
        n = (last - lead) * 64
        for b in range(lead, last):
            far = gath.at[b, xo]
            remote(far.at[:, lo], far.at[:, lo], gsend.at[b, 2], grecv.at[b, 2], right).wait_recv()
            remote(far.at[:, hi], far.at[:, hi], gsend.at[b, 3], grecv.at[b, 3], left).wait_recv()
        rows = gath[lead:last].reshape(n, d)
        base = rows[:, 0:1].astype(F32)
        total, squares = jnp.zeros((n, 128), F32), jnp.zeros((n, 128), F32)
        for k in range(d // 128):
            e = rows[:, k * 128:(k + 1) * 128].astype(F32) - base
            total, squares = total + e, squares + e * e
        off = jnp.sum(total, axis=1, keepdims=True) * (1.0 / d)
        spread = jnp.sum(squares, axis=1, keepdims=True) * (1.0 / d) - off * off
        scale = lax.rsqrt(spread + 1e-06)
        mean = base + off
        for k in range(d // 128):
            cols = slice(k * 128, (k + 1) * 128)
            center = (rows[:, cols].astype(F32) - mean) * scale
            tnorm[0:n, cols] = (center * (1.0 + tmod[1:2, cols]) + tmod[0:1, cols]).astype(BF)
        if lead == 0:
            weight_end(1)
        joined = dot(tnorm[0:n], wt[...].reshape(d, 1536)).astype(BF)
        same = (iota((n, n), 0) >> 3) == (iota((n, n), 1) >> 3)
        attended = []
        for j in range(4):
            mine = joined[:, j * 384:(j + 1) * 384]
            scores = jnp.where(same, dot_nt(mine[:, 0:128], mine[:, 128:256]), -1e30)
            top = jnp.max(scores, axis=1, keepdims=True)
            probs = jnp.exp2((scores - top) * score_scale)
            probs = (probs / jnp.sum(probs, axis=1, keepdims=True)).astype(BF)
            attended.append(dot(probs, mine[:, 256:384]).astype(BF))
        if lead == 0:
            weight_end(2)
        lhs = jnp.concatenate(attended, axis=1)
        for half, cols in ((0, lo), (1, hi)):
            some = dot(lhs, wto[:, :, :, :, cols].reshape(512, hb)).astype(BF)
            part2[lead:last, :, :, cols] = some.reshape(last - lead, 4, 16, hb)
            for b in range(lead, last):
                ring_first(b, half, part2, relay2, got2, rsend2, rrecv2)

    def back_second(b):
        ring_second(b, part2, relay2, got2, rsend2, rrecv2)

    def finish(b):
        total = ring_last(b, part2, got2, rsend2, rrecv2)
        res[b] = (gath[b, x].astype(F32) + tmod[2:3, :] * total).astype(BF)
        rows = pl.ds(pl.multiple_of(b * 16, 16), 16)
        pltpu.make_async_copy(res.at[b], out.at[rows, :], out_sem.at[b]).start()

    def sum_second(b):
        ring_second(b, part, relay, got, rsend, rrecv)

    def sent(b, _):
        for r in (1, 2, 3):
            remote(cat.at[b, r], cat.at[b, r], asend.at[b, r], arecv.at[b, r], quad[r]).wait_send()
        ring_sent(b, relay, rsend, rrecv)
        for j in range(1, 8):
            piece = shuf.at[b, 0]
            remote(piece, piece, ssend.at[b, j], srecv.at[b, j], right).wait_send()
        for k in range(4):
            piece = gath.at[b, x] if k < 2 else gath.at[b, x, :, lo]
            remote(piece, piece, gsend.at[b, k], grecv.at[b, k], right).wait_send()
        return 0

    def drain():
        lax.fori_loop(0, nb, sent, 0)
        for w in range(3):
            weight_sent(w)

    blocks = {
        "attend": attend, "sum_begin": sum_begin, "sum_second": sum_second, "swap_send": swap_send,
        "gather_send": gather_send, "gather_relay": gather_relay, "back_second": back_second, "finish": finish,
    }
    moves = {"temporal": temporal, "quarter": weight_quarter, "relay": weight_relay, "rest": weight_rest,
        "drain": drain}

    def tick(t, _):
        for name, *what in TABLE:
            if name in blocks:
                hit, b = t < 0, 0
                for when, block in what:
                    hit = hit | (t == when)
                    b = b + jnp.where(t == when, block, 0)

                @pl.when(hit)
                def _(name=name, b=b):
                    blocks[name](b)
            else:
                @pl.when(t == what[0])
                def _(name=name, what=what):
                    moves[name](*what[1:])

        return 0

    lax.fori_loop(0, COUNT, tick, 0)

    for b in range(nb):
        pltpu.make_async_copy(res.at[b], out.at[pl.ds(b * 16, 16), :], out_sem.at[b]).wait()

    def back_sent(b, _):
        ring_sent(b, relay2, rsend2, rrecv2)
        return 0

    lax.fori_loop(0, nb, back_sent, 0)


def shards(
    tokens, spatial_modulation, spatial_weights_in, spatial_weights_out,
    temporal_modulation, temporal_weights_in, temporal_weights_out,
):
    d = tokens.shape[-1]
    nb = BLOCKS
    hb = d // 2
    dma = pltpu.SemaphoreType.DMA
    any_space = pl.BlockSpec(memory_space=pl.ANY)
    vmem = pl.BlockSpec(memory_space=pltpu.VMEM)
    out_weights = pltpu.VMEM((4, 4, 2, 16, d), BF)
    ring = [
        pltpu.VMEM((nb, 4, 16, d), BF),
        pltpu.VMEM((nb, 2, 16, hb), BF),
        pltpu.VMEM((nb, 2, 2, 16, hb), BF),
    ]
    result = pl.pallas_call(
        kernel,
        out_shape=jax.ShapeDtypeStruct((80, d), BF),
        in_specs=[any_space, vmem, any_space, any_space, vmem, any_space, any_space],
        out_specs=any_space,
        scratch_shapes=[
            pltpu.VMEM((4, 336, d), BF),
            pltpu.VMEM((16, d), BF),
            pltpu.VMEM((d, 384), BF),
            pltpu.VMEM((d, 512), BF),
            pltpu.VMEM((1280, 128), BF),
            pltpu.VMEM((1280, 128), BF),
            pltpu.VMEM((1280, 256), BF),
            pltpu.VMEM((nb, 4, 64, 128), BF),
            pltpu.VMEM((nb, 4, 64, 128), BF),
            pltpu.VMEM((80, d), BF),
            out_weights,
            pltpu.VMEM((4, 4, d // 16, 1536), BF),
            out_weights,
            *ring,
            pltpu.VMEM((nb, 8, 16, d // 8), BF),
            pltpu.VMEM((nb, 8, 16, d // 8), BF),
            pltpu.VMEM((nb, 4, 16, d), BF),
            pltpu.VMEM((nb * 64, d), BF),
            *ring,
            pltpu.VMEM((nb, 16, d), BF),
            dma((3,)), dma((4,)), dma((nb,)), dma(()),
            dma((3, 9, 4)), dma((3, 9, 4)),
            dma((nb, 4)), dma((nb, 4)),
            dma((nb, 6)), dma((nb, 6)),
            dma((nb, 8)), dma((nb, 8)),
            dma((nb, 4)), dma((nb, 4)),
            dma((nb, 6)), dma((nb, 6)),
        ],
        compiler_params=pltpu.CompilerParams(
            collective_id=0, has_side_effects=True, vmem_limit_bytes=60 * 1024 * 1024
        ),
        cost_estimate=pl.CostEstimate(
            flops=9_000_000_000, bytes_accessed=16_000_000, transcendentals=2_000_000
        ),
    )(
        tokens.reshape(4, 320, d),
        spatial_modulation,
        jnp.transpose(spatial_weights_in, (1, 0, 2)).reshape(d, 384),
        spatial_weights_out.reshape(4, 2, 16, d),
        temporal_modulation,
        jnp.transpose(temporal_weights_in, (1, 0, 2)).reshape(4, 4, d // 16, 384),
        temporal_weights_out.reshape(4, 2, 16, d),
    )
    return jnp.transpose(result.reshape(10, 8, d), (1, 0, 2))


def solution(mesh):
    placed = (
        P("seq", None, None),
        P(),
        P(None, "head", None),
        P("head", None, None),
        P(),
        P(None, "head", None),
        P("head", None, None),
    )
    return jax.shard_map(
        shards,
        mesh=mesh,
        in_specs=placed,
        out_specs=P(None, ("seq", "head"), None),
        check_vma=False,
    )
```
